512 devices in a mesh: alt: 8 (over x, y_hi), strip: 64 (over z, y_lo, core).
Axes of the slice: x: 4, y: 4 (y_hi: 2, y_lo: 2; y = y_hi * 2 + y_lo), z: 16, core: 2. Of those that a mesh axis runs over, the one named last changes fastest.
Arguments:
- screens: bfloat16 [16, 512, 512], P('alt', 'strip'), may hold values from -2.390625 to 2.390625
- row_offset: int32 [2, 16, 2], replicated, may hold values from 0 to 341, as said below
- col_offset: int32 [2, 16, 2], replicated, may hold values from 0 to 341, as said below
- layer_bin: int32 [16], replicated, may hold values from 0 to 15
- illumination: float32 [16, 12800], P(None, ('alt', 'strip')), may hold values from 0.3 to 1
- reconstructor: bfloat16 [2, 12800, 6000], P(None, ('alt', 'strip')), may hold values from -0.0390625 to 0.0390625
- sat_code: int32 [6000], replicated, may hold values from 1 to 16
Outputs:
- slopes: float32 [2, 2, 12800], P(None, None, ('alt', 'strip'))
- commands: float32 [2, 6000], replicated
The draws below stay inside these ranges and needn't reach their ends.
Inputs may be any that keep to these rules, and one draw needn't show every extreme that they name: Every footprint lies inside the screen: row_offset[f, l, g] + (319) shrink_l <= 511. Every footprint lies inside the screen: col_offset[f, l, g] + (319) shrink_l <= 511.
All inputs are finite; a program needn't handle non-finite values.
Results may differ from the reference program's by a relative error of at most 0.0028.
Values sent between devices are 32-bit elements; how exact they have to be, the bound alone decides.
No kernel may reach another device: no remote copies, remote signals or barrier semaphores. Data moves between devices by JAX's collectives and lax.ppermute only.
A program may use at most 64 MiB of HBM per device.

```python
import math
import jax
import jax.numpy as jnp
from jax import lax

LENSLETS = 80
PIXELS = 4
GUIDE_STARS = 2
FRAMES = 2
ACTUATORS = 6000
SCREEN_ROWS = 512
COLUMNS = 512
LAYERS = 16
PUPIL_PIX = 320
WINDOW = 384
SUBAPS_ALL = 12800


def geometry(key):
    base = jax.random.fold_in(key, 7013)
    keys = jax.random.split(base, 6)
    bins = jax.random.randint(keys[0], (LAYERS,), 0, 16, dtype=jnp.int32)
    order = jax.random.permutation(keys[1], LAYERS)
    bins = bins.at[order[0]].set(0).at[order[1]].set(15)
    stars = jnp.arange(GUIDE_STARS, dtype=jnp.int32)
    pattern = (2 * stars - (GUIDE_STARS - 1)) * 3 // (GUIDE_STARS - 1)
    dir_rows = jax.random.permutation(keys[2], pattern)
    dir_cols = jax.random.permutation(keys[3], pattern)
    wind_reach_rows = max(1, (SCREEN_ROWS - PUPIL_PIX) // 48)
    wind_reach_cols = max(1, (COLUMNS - PUPIL_PIX) // 48)
    wind_rows = jax.random.randint(keys[4], (LAYERS,), -wind_reach_rows, wind_reach_rows + 1, dtype=jnp.int32)
    wind_cols = jax.random.randint(keys[5], (LAYERS,), -wind_reach_cols, wind_reach_cols + 1, dtype=jnp.int32)
    return (bins, dir_rows, dir_cols, wind_rows, wind_cols)


def placement(bins, directions, winds, extent):
    half_span = (PUPIL_PIX - 1) * (32 - bins) // 64
    full_span = ((PUPIL_PIX - 1) * (32 - bins) + 31) // 32
    displaced = directions[None, :] * bins[:, None] * (extent - PUPIL_PIX) // 32
    first = extent // 2 - half_span[:, None] + displaced
    frame_steps = jnp.arange(FRAMES, dtype=jnp.int32)
    starts = first[None, :, :] + frame_steps[:, None, None] * winds[None, :, None]
    upper = extent - 1 - full_span
    return jnp.clip(starts, 0, upper[None, :, None]).astype(jnp.int32)


def draw_layer_bin(key, part):
    bins, dir_rows, dir_cols, wind_rows, wind_cols = geometry(key)
    return bins.astype(jnp.int32)


def draw_row_offset(key, part):
    bins, dir_rows, dir_cols, wind_rows, wind_cols = geometry(key)
    return placement(bins, dir_rows, wind_rows, SCREEN_ROWS)


def draw_col_offset(key, part):
    bins, dir_rows, dir_cols, wind_rows, wind_cols = geometry(key)
    return placement(bins, dir_cols, wind_cols, COLUMNS)


def place_ends(result, key, low, top_value):
    place = [jax.random.randint(jax.random.fold_in(key, axis), (), 0, length) for axis, length in enumerate(result.shape)]
    longest = result.shape.index(max(result.shape))
    next_to = place[:longest] + [(place[longest] + 1) % result.shape[longest]] + place[longest + 1:]
    return result.at[tuple(place)].set(low).at[tuple(next_to)].set(top_value)


def block_levels(stream_key, shape, cuts, smallest, high):
    factor_of = 1.0
    for dim, shards_of in cuts:
        steps = jax.random.uniform(jax.random.fold_in(jax.random.fold_in(stream_key, 6), dim), (shards_of,), jnp.float32, smallest / len(cuts), high / len(cuts))
        factor_of = factor_of * jnp.repeat(jnp.exp(steps), shape[dim] // shards_of).reshape((-1,) + (1,) * (len(shape) - 1 - dim))
    return factor_of


def noise(rng, dims, deviation, reach, cuts=(), kind=jnp.bfloat16):
    entries = jax.random.normal(rng, dims, jnp.float32) * deviation
    if len(cuts) > 0:
        entries = block_levels(rng, dims, cuts, -0.22, 0.18) * entries
    return jnp.clip(entries, min=-reach, max=reach).astype(kind)


def setup_inputs(seed: int = 0) -> dict:
    arg_keys = jax.random.split(jax.random.key(seed), 8)
    screens = noise(arg_keys[0], (LAYERS, SCREEN_ROWS, COLUMNS), 0.3, 2.390625, ((0, 8), (1, 64)))
    row_offset = draw_row_offset(jax.random.fold_in(arg_keys[7], 71), 0)
    col_offset = draw_col_offset(jax.random.fold_in(arg_keys[7], 71), 0)
    layer_bin = draw_layer_bin(jax.random.fold_in(arg_keys[7], 71), 0)
    illumination = jnp.clip(jnp.exp(math.log(1.0) - 1.2039728 * jax.random.uniform(arg_keys[4], (PIXELS * PIXELS, SUBAPS_ALL), jnp.float32) ** block_levels(arg_keys[4], (PIXELS * PIXELS, SUBAPS_ALL), ((1, 512),), -0.2, 0.2)), 0.3, 1.0)
    reconstructor = noise(arg_keys[5], (2, SUBAPS_ALL, ACTUATORS), (2 * SUBAPS_ALL) ** -0.5, 0.0390625, ((1, 512),))
    sat_code = place_ends(jax.random.randint(arg_keys[6], (ACTUATORS,), 1, 17), jax.random.fold_in(arg_keys[6], 1), 1, 16).astype(jnp.int32)
    return dict(screens=screens, row_offset=row_offset, col_offset=col_offset, layer_bin=layer_bin, illumination=illumination, reconstructor=reconstructor, sat_code=sat_code)


highest = lax.Precision.HIGHEST
loop_gain = 0.5
code_step = 0.125
bin_step = 0.03125


def bilinear(offsets):
    return jnp.maximum(0.0, 1.0 - jnp.abs(offsets))


def dft_tables():
    padded = 2 * PIXELS
    freq_index = jnp.arange(padded * padded, dtype=jnp.int32)
    freq_row = freq_index // padded
    freq_col = freq_index % padded
    pix_index = jnp.arange(PIXELS * PIXELS, dtype=jnp.int32)
    pix_row = pix_index // PIXELS
    pix_col = pix_index % PIXELS
    turn_count = (freq_row[:, None] * pix_row[None, :] + freq_col[:, None] * pix_col[None, :]) % padded
    angles = turn_count.astype(jnp.float32) * (2.0 * math.pi / padded)
    coord_row = ((freq_row + PIXELS) % padded - PIXELS).astype(jnp.float32)
    coord_col = ((freq_col + PIXELS) % padded - PIXELS).astype(jnp.float32)
    return jnp.cos(angles), jnp.sin(angles), coord_row, coord_col


def centroids(pupil_phase, illumination, tables):
    cosine, sine_table, coord_row, coord_col = tables
    field_re = illumination * jnp.cos(pupil_phase)
    field_im = illumination * jnp.sin(pupil_phase)
    real_part = jnp.dot(cosine, field_re, precision=highest) + jnp.dot(sine_table, field_im, precision=highest)
    imag_part = jnp.dot(cosine, field_im, precision=highest) - jnp.dot(sine_table, field_re, precision=highest)
    intensity = real_part * real_part + imag_part * imag_part
    flux_sum = jnp.sum(intensity, axis=0)
    slope_row = jnp.sum(intensity * coord_row[:, None], axis=0) / flux_sum
    slope_col = jnp.sum(intensity * coord_col[:, None], axis=0) / flux_sum
    return jnp.stack([slope_row, slope_col])


def project_frame(screens, row_start, col_start, shrinks):
    pupil_idx = jnp.arange(PUPIL_PIX, dtype=jnp.float32)
    window_idx = jnp.arange(WINDOW, dtype=jnp.float32)

    def one_layer(running, inputs):
        screen, tops, lefts, shrink = inputs
        widened = jnp.pad(screen, ((0, WINDOW), (0, WINDOW)))
        weights = bilinear(window_idx[None, :] - pupil_idx[:, None] * shrink)

        def one_star(top_row, left_col):
            window_block = lax.dynamic_slice(widened, (top_row, left_col), (WINDOW, WINDOW)).astype(jnp.float32)
            across = jnp.dot(window_block, weights.T, precision=highest)
            return jnp.dot(weights, across, precision=highest)

        return running + jax.vmap(one_star)(tops, lefts), None

    initial = jnp.zeros((GUIDE_STARS, PUPIL_PIX, PUPIL_PIX), jnp.float32)
    summed, unused = lax.scan(one_layer, initial, (screens, row_start, col_start, shrinks))
    return summed


def reference(screens, row_offset, col_offset, layer_bin, illumination, reconstructor, sat_code):
    shrinks = 1.0 - layer_bin.astype(jnp.float32) * bin_step
    tables = dft_tables()
    slope_list = []
    for frame_no in range(FRAMES):
        summed = project_frame(screens, row_offset[frame_no], col_offset[frame_no], shrinks)
        pupil_phase = summed.reshape(GUIDE_STARS, LENSLETS, PIXELS, LENSLETS, PIXELS)
        pupil_phase = pupil_phase.transpose(2, 4, 0, 1, 3).reshape(PIXELS * PIXELS, SUBAPS_ALL)
        slope_list.append(centroids(pupil_phase, illumination, tables))
    slopes = jnp.stack(slope_list)
    rounded = slopes.astype(jnp.bfloat16).reshape(FRAMES, 2 * SUBAPS_ALL)
    updates = jnp.dot(rounded, reconstructor.reshape(2 * SUBAPS_ALL, ACTUATORS), preferred_element_type=jnp.float32)
    limits = sat_code.astype(jnp.float32) * code_step
    first_cmd = jnp.clip(loop_gain * updates[0], -limits, limits)
    second_cmd = jnp.clip(first_cmd + loop_gain * updates[1], -limits, limits)
    return slopes, jnp.stack([first_cmd, second_cmd])
```

```python
import jax
import jax.numpy as jnp
from jax import lax
from jax.experimental import pallas as pl
from jax.experimental.pallas import tpu as pltpu
from jax.sharding import Mesh, PartitionSpec as P

ACTUATORS = 6000
F32 = jnp.float32
BF16 = jnp.bfloat16
I32 = jnp.int32

NAMES = ("xh", "xl", "yh", "zh", "zl", "yl", "co")
SIZES = (2, 2, 2, 4, 4, 2, 2)
ALT = ("xh", "xl", "yh")
STRIP = ("zh", "zl", "yl", "co")
PLANE = ("xh", "xl", "yh", "yl", "co")
HALF = ("xl", "yh", "yl", "co")
RING = ("zh", "zl")

ROOT = 2.0**0.5
LAG = (2.0 + 2.0 * ROOT, -2.0, 2.0 * ROOT - 2.0)

SMEM = pl.BlockSpec(memory_space=pltpu.SMEM)
VMEM = pl.BlockSpec(memory_space=pltpu.VMEM)


def iota(shape, dim):
    return lax.broadcasted_iota(I32, shape, dim)


def alt_index():
    return lax.axis_index("xh") * 4 + lax.axis_index("xl") * 2 + lax.axis_index("yh")


def ylc_index():
    return lax.axis_index("yl") * 2 + lax.axis_index("co")


def block_index():
    return (lax.axis_index("xl") * 2 + lax.axis_index("yh")) * 4 + ylc_index()


def columns_kernel(col_ref, bin_ref, screen_ref, out_ref):
    alt = alt_index()
    lane = iota((1, 512), 1)
    column = (4 * (5 * (lane >> 5) + (lane & 7)) + ((lane >> 3) & 3)).astype(F32)
    position = iota((384, 512), 0).astype(F32)
    results = []
    for layer in range(2):
        where = alt * 2 + layer
        shrink = 1.0 - bin_ref[where].astype(F32) * 0.03125
        weights = jnp.maximum(0.0, 1.0 - jnp.abs(position - column * shrink)).astype(BF16)
        rows = screen_ref[layer].astype(F32)
        parts = []
        for frame in range(2):
            for star in range(2):
                left = col_ref[frame, where, star]
                turned = pltpu.roll(rows, lax.rem(512 - left, 512), axis=1)
                parts.append(turned[:, :384])
        stacked = jnp.concatenate(parts, axis=0).astype(BF16)
        results.append(jnp.dot(stacked, weights, preferred_element_type=F32))
    group = iota((8, 128), 1) >> 5
    for star in range(2):
        for tile in range(4):
            slots = []
            for layer in range(2):
                for frame in range(2):
                    top = (frame * 2 + star) * 8
                    slots.append(results[layer][top : top + 8, tile * 128 : tile * 128 + 128])
            for inner in range(4):
                merged = jnp.zeros((8, 128), F32)
                for slot in range(4):
                    shift = (32 * (slot - inner)) % 128
                    moved = slots[slot] if shift == 0 else pltpu.roll(slots[slot], shift, axis=1)
                    merged = jnp.where(group == slot, moved, merged)
                out_ref[star * 16 + tile * 4 + inner] = merged


def rows_kernel(row_ref, bin_ref, got_ref, out_ref):
    star = lax.axis_index("xh")
    block = block_index()
    ring = lax.axis_index("zh") * 4 + lax.axis_index("zl")
    values = got_ref[...].reshape(256, 128)
    high = values.astype(BF16).astype(F32)
    low = values - high
    lane = iota((256, 128), 1)
    line = iota((256, 1), 0)
    z_to = line >> 4
    quarter = (line >> 2) & 3
    zl = z_to & 3
    first = (20 * zl - block + 15) >> 4
    pupil_row = (4 * (20 * quarter + 5 * (z_to >> 2) + first) + (line & 3)).astype(F32)
    cell = iota((1, 256), 1)
    owner = cell >> 5
    screen_row = ring * 32 + (cell & 31)
    sums = [jnp.zeros((256, 128), F32), jnp.zeros((256, 128), F32)]
    for layer in range(2):
        shrink = jnp.zeros((1, 256), F32)
        for alt in range(8):
            value = 1.0 - bin_ref[alt * 2 + layer].astype(F32) * 0.03125
            shrink = jnp.where(owner == alt, value, shrink)
        scaled = [pupil_row * shrink, (pupil_row + 4.0) * shrink]
        for frame in range(2):
            top = jnp.zeros((1, 256), I32)
            for alt in range(8):
                top = jnp.where(owner == alt, row_ref[frame, alt * 2 + layer, star], top)
            offset = (screen_row - top).astype(F32)
            slot = layer * 2 + frame
            shift = (64 * frame - 32 * slot) % 128
            moved = high if shift == 0 else pltpu.roll(high, shift, axis=1)
            shift = (64 * frame + 32 - 32 * slot) % 128
            other = low if shift == 0 else pltpu.roll(low, shift, axis=1)
            part = lane >> 5
            right = jnp.where(part == 2 * frame, moved, jnp.where(part == 2 * frame + 1, other, 0.0)).astype(BF16)
            for half in range(2):
                weights = jnp.maximum(0.0, 1.0 - jnp.abs(offset - scaled[half])).astype(BF16)
                sums[half] = sums[half] + jnp.dot(weights, right, preferred_element_type=F32)
    zero = sums[0] + pltpu.roll(sums[0], 96, axis=1)
    one = sums[1] + pltpu.roll(sums[1], 32, axis=1)
    out_ref[...] = jnp.where((lane & 63) < 32, zero, one).reshape(16, 16, 128)


def spread_kernel(got_ref, out_ref):
    total = jnp.sum(got_ref[...], axis=0)
    for quarter in range(4):
        top = (quarter // 2) * 8
        for ylc in range(4):
            out_ref[quarter * 4 + ylc] = total[top : top + 8]


def slopes_kernel(got_ref, light_ref, recon_ref, slopes_ref, out_ref, scratch):
    zl = lax.axis_index("zl")
    yh = lax.axis_index("yh")
    ylc = ylc_index()
    row = iota((8, 128), 0)
    lane = iota((8, 128), 1)
    cell = (lane & 63) >> 3
    phases = [jnp.zeros((8, 128), F32), jnp.zeros((8, 128), F32)]
    for i in range(5):
        flat = 20 * zl + 5 * ylc + i
        source = flat & 15
        slot = (flat >> 4) - ((20 * zl - source + 15) >> 4)
        block = got_ref[source]
        both = jnp.where((row >> 2) == yh, block, pltpu.roll(block, 4, axis=0))
        turned = []
        for q in range(4):
            shift = lax.rem(256 + 8 * i - 32 * slot - 8 * q, 128)
            turned.append(pltpu.roll(both, shift, axis=1))
        for h in range(2):
            pair = jnp.where(row < 4, turned[2 * h], turned[2 * h + 1])
            phases[h] = jnp.where(cell == i, pair, phases[h])
    scratch[...] = jnp.zeros((16, 128), F32)
    scratch[:, 0:25] = light_ref[...]
    wide = scratch[...]
    lane16 = iota((16, 128), 1)
    placed = jnp.ones((16, 128), F32)
    for frame in range(2):
        for i in range(5):
            shift = 64 * frame + 3 * i
            moved = wide if shift == 0 else pltpu.roll(wide, shift, axis=1)
            start = 64 * frame + 8 * i
            placed = jnp.where((lane16 >= start) & (lane16 < start + 5), moved, placed)
    scratch[...] = placed
    re, im = [], []
    for h in range(2):
        light = jnp.concatenate(
            [scratch[pl.ds(2 * h, 4, stride=4), :], scratch[pl.ds(2 * h + 1, 4, stride=4), :]], axis=0
        )
        re.append(light * jnp.cos(phases[h]))
        im.append(light * jnp.sin(phases[h]))
    power = re[0] * re[0] + im[0] * im[0] + re[1] * re[1] + im[1] * im[1]
    flux = jnp.sum(power, axis=0, keepdims=True)
    along_p = -4.0 * power
    pixel = row & 3
    for h in range(2):
        for d in range(1, 4):
            back_re = pltpu.roll(re[h], d, axis=0)
            back_im = pltpu.roll(im[h], d, axis=0)
            same = re[h] * back_re + im[h] * back_im
            cross = im[h] * back_re - re[h] * back_im
            sign = -8.0 if d % 2 == 0 else 8.0
            term = sign * same + (4.0 * LAG[d - 1]) * cross
            along_p = along_p + jnp.where(pixel >= d, term, 0.0)
    swap_re = [pltpu.roll(x, 4, axis=0) for x in re]
    swap_im = [pltpu.roll(x, 4, axis=0) for x in im]

    def term_of(to_re, to_im, from_re, from_im, d):
        same = to_re * from_re + to_im * from_im
        cross = to_im * from_re - to_re * from_im
        sign = -8.0 if d % 2 == 0 else 8.0
        return sign * same + (4.0 * LAG[d - 1]) * cross

    along_q = -4.0 * power
    upper = row >= 4
    for h in range(2):
        along_q = along_q + jnp.where(upper, term_of(re[h], im[h], swap_re[h], swap_im[h], 1), 0.0)
    along_q = along_q + term_of(re[1], im[1], re[0], im[0], 2)
    near = term_of(re[1], im[1], swap_re[0], swap_im[0], 1)
    far = term_of(re[1], im[1], swap_re[0], swap_im[0], 3)
    along_q = along_q + jnp.where(upper, far, near)
    scale = 0.125 / flux
    slope_p = jnp.sum(along_p, axis=0, keepdims=True) * scale
    slope_q = jnp.sum(along_q, axis=0, keepdims=True) * scale
    pair = jnp.where(row == 0, slope_p, slope_q)
    compact = []
    for frame in range(2):
        packed = jnp.zeros((8, 128), F32)
        for i in range(5):
            shift = (-64 * frame - 3 * i) % 128
            moved = pair if shift == 0 else pltpu.roll(pair, shift, axis=1)
            packed = jnp.where((lane >= 5 * i) & (lane < 5 * i + 5), moved, packed)
        compact.append(packed)
        slopes_ref[frame] = packed[0:2, 0:25]
    total = jnp.zeros((8, ACTUATORS), F32)
    for axis in range(2):
        left = jnp.where(row == 0, compact[0][axis : axis + 1], compact[1][axis : axis + 1])
        left = left[:, 0:25].astype(BF16)
        total = total + jnp.dot(left, recon_ref[axis], preferred_element_type=F32)
    for j in range(23):
        out_ref[j] = total[0:2, 256 * j : 256 * j + 256]
    out_ref[23] = jnp.zeros((2, 256), F32)
    out_ref[23, :, 0:112] = total[0:2, 5888:6000]
    for j in range(24, 32):
        out_ref[j] = jnp.zeros((2, 256), F32)


def sum_kernel(got_ref, out_ref):
    total = jnp.sum(got_ref[...], axis=0)
    for i in range(out_ref.shape[0]):
        out_ref[i] = total


def clip_kernel(got_ref, code_ref, out_ref):
    for j in range(24):
        width = 256 if j < 23 else 112
        update = got_ref[j][:, 0:width]
        limit = code_ref[:, 256 * j : 256 * j + width].astype(F32) * 0.125
        first = jnp.clip(0.5 * update[0:1], -limit, limit)
        second = jnp.clip(first + 0.5 * update[1:2], -limit, limit)
        out_ref[0:1, 256 * j : 256 * j + width] = first
        out_ref[1:2, 256 * j : 256 * j + width] = second


def call(body, outs, specs, *args, scratch=(), name=None):
    return pl.pallas_call(
        body,
        out_shape=outs,
        in_specs=specs,
        out_specs=jax.tree.map(lambda _: VMEM, outs),
        scratch_shapes=list(scratch),
        compiler_params=pltpu.CompilerParams(vmem_limit_bytes=16 * 1024 * 1024),
        name=name,
    )(*args)


def exchange(value, axes):
    return lax.all_to_all(value, axes, 0, 0, tiled=True)


def shards(screens, row_offset, col_offset, layer_bin, illumination, reconstructor, sat_code):
    shape = jax.ShapeDtypeStruct
    cols = call(columns_kernel, shape((32, 8, 128), F32), [SMEM, SMEM, VMEM], col_offset, layer_bin, screens, name="columns")
    cols = exchange(cols, PLANE)
    pupil = call(rows_kernel, shape((16, 16, 128), F32), [SMEM, SMEM, VMEM], row_offset, layer_bin, cols, name="rows")
    pupil = exchange(pupil, RING)
    owned = call(spread_kernel, shape((16, 8, 128), F32), [VMEM], pupil, name="spread")
    owned = exchange(owned, HALF)
    slopes, updates = call(
        slopes_kernel,
        (shape((2, 2, 25), F32), shape((32, 2, 256), F32)),
        [VMEM, VMEM, VMEM],
        owned,
        illumination,
        reconstructor,
        scratch=[pltpu.VMEM((16, 128), F32)],
        name="slopes",
    )
    updates = exchange(updates, PLANE)
    updates = call(sum_kernel, shape((16, 2, 256), F32), [VMEM], updates, name="sum_plane")
    updates = exchange(updates, RING)
    updates = call(sum_kernel, shape((32, 2, 256), F32), [VMEM], updates, name="sum_ring")
    updates = exchange(updates, PLANE)
    commands = call(
        clip_kernel, shape((2, ACTUATORS), F32), [VMEM, VMEM], updates, sat_code.reshape(1, ACTUATORS), name="clip"
    )
    return slopes, commands


def solution(mesh):
    fine = Mesh(mesh.devices.reshape(SIZES), NAMES)
    placed = (
        P(ALT, STRIP, None),
        P(),
        P(),
        P(),
        P(None, ALT + STRIP),
        P(None, ALT + STRIP, None),
        P(),
    )
    return jax.shard_map(
        shards,
        mesh=fine,
        in_specs=placed,
        out_specs=(P(None, None, ALT + STRIP), P()),
        check_vma=False,
    )
```

```python
import jax
import jax.numpy as jnp
from jax import lax
from jax.experimental import pallas as pl
from jax.experimental.pallas import tpu as pltpu
from jax.sharding import Mesh, PartitionSpec as P

ACTUATORS = 6000
F32 = jnp.float32
BF16 = jnp.bfloat16
I32 = jnp.int32

NAMES = ("xh", "xl", "yh", "zh", "zl", "yl", "co")
SIZES = (2, 2, 2, 4, 4, 2, 2)
ALT = ("xh", "xl", "yh")
STRIP = ("zh", "zl", "yl", "co")
PLANE = ("xh", "xl", "yh", "yl", "co")
HALF = ("xl", "yh", "yl", "co")
RING = ("zh", "zl")

ROOT = 2.0**0.5
LAG = (2.0 + 2.0 * ROOT, -2.0, 2.0 * ROOT - 2.0)

SMEM = pl.BlockSpec(memory_space=pltpu.SMEM)
VMEM = pl.BlockSpec(memory_space=pltpu.VMEM)


def iota(shape, dim):
    return lax.broadcasted_iota(I32, shape, dim)


def alt_index():
    return lax.axis_index("xh") * 4 + lax.axis_index("xl") * 2 + lax.axis_index("yh")


def ylc_index():
    return lax.axis_index("yl") * 2 + lax.axis_index("co")


def block_index():
    return (lax.axis_index("xl") * 2 + lax.axis_index("yh")) * 4 + ylc_index()


def columns_kernel(col_ref, bin_ref, screen_ref, out_ref):
    alt = alt_index()
    lane = iota((1, 512), 1)
    block = lane >> 5
    part = (lane & 31) >> 2
    lenslet = jnp.where(part < 4, 20 * part + block, 20 * (block >> 2) + 16 + (block & 3))
    column = (4 * lenslet + (lane & 3)).astype(F32)
    position = iota((384, 512), 0).astype(F32)
    results = []
    for layer in range(2):
        where = alt * 2 + layer
        shrink = 1.0 - bin_ref[where].astype(F32) * 0.03125
        weights = jnp.maximum(0.0, 1.0 - jnp.abs(position - column * shrink)).astype(BF16)
        rows = screen_ref[layer].astype(F32)
        parts = []
        for frame in range(2):
            for star in range(2):
                left = col_ref[frame, where, star]
                turned = pltpu.roll(rows, lax.rem(512 - left, 512), axis=1)
                parts.append(turned[:, :384])
        stacked = jnp.concatenate(parts, axis=0).astype(BF16)
        results.append(jnp.dot(stacked, weights, preferred_element_type=F32))
    group = iota((8, 128), 1) >> 5
    for star in range(2):
        for tile in range(4):
            slots = []
            for layer in range(2):
                for frame in range(2):
                    top = (frame * 2 + star) * 8
                    slots.append(results[layer][top : top + 8, tile * 128 : tile * 128 + 128])
            for inner in range(4):
                merged = jnp.zeros((8, 128), F32)
                for slot in range(4):
                    shift = (32 * (slot - inner)) % 128
                    moved = slots[slot] if shift == 0 else pltpu.roll(slots[slot], shift, axis=1)
                    merged = jnp.where(group == slot, moved, merged)
                out_ref[star * 16 + tile * 4 + inner] = merged


def rows_kernel(row_ref, bin_ref, light_ref, got_ref, out_ref, light_out, scratch):
    star = lax.axis_index("xh")
    block = block_index()
    ring = lax.axis_index("zh") * 4 + lax.axis_index("zl")
    values = got_ref[...].reshape(256, 128)
    high = values.astype(BF16).astype(F32)
    low = values - high
    wide = iota((256, 128), 1)
    rights = [
        jnp.where(wide < 64, high, pltpu.roll(low, 64, axis=1)).astype(BF16),
        jnp.where(wide < 64, pltpu.roll(high, 64, axis=1), low).astype(BF16),
    ]
    line = iota((64, 1), 0)
    base = (80 * ((line >> 2) & 3) + 20 * (line >> 4) + (line & 3)).astype(F32)
    pupil_row = jnp.concatenate([base + 4.0 * rr for rr in range(5)], axis=0)
    cell = iota((1, 256), 1)
    owner = cell >> 5
    screen_row = ring * 32 + (cell & 31)
    sums = [None, None]
    for layer in range(2):
        shrink = jnp.zeros((1, 256), F32)
        for alt in range(8):
            value = 1.0 - bin_ref[alt * 2 + layer].astype(F32) * 0.03125
            shrink = jnp.where(owner == alt, value, shrink)
        scaled = pupil_row * shrink
        for frame in range(2):
            top = jnp.zeros((1, 256), I32)
            for alt in range(8):
                top = jnp.where(owner == alt, row_ref[frame, star, alt * 2 + layer], top)
            offset = (screen_row - top).astype(F32)
            weights = jnp.maximum(0.0, 1.0 - jnp.abs(offset - scaled)).astype(BF16)
            term = jnp.dot(weights, rights[layer], preferred_element_type=F32)
            sums[frame] = term if layer == 0 else sums[frame] + term
    lane = iota((8, 128), 1)
    cell = lane & 31
    odd = (lane & 32) != 0
    kind = jnp.where(cell < 16, cell >> 2, block >> 2)
    for t in range(4):
        pieces = []
        for rr in range(5):
            halves = []
            for h in range(2):
                start = rr * 64 + t * 16 + h * 8
                both = jnp.where(odd, sums[1][start : start + 8], sums[0][start : start + 8])
                halves.append(both + pltpu.roll(both, 64, axis=1))
            pieces.append(jnp.where(lane < 64, halves[0], halves[1]))
        for zl in range(4):
            here, after = pieces[zl], pieces[zl + 1]
            first = jnp.where(kind < zl, after, here)
            second = jnp.where(cell < 24, pltpu.roll(after, 20 - 4 * zl, axis=1), pltpu.roll(after, 8, axis=1))
            out_ref[t * 4 + zl] = jnp.where(cell < 20, first, second)
    scratch[...] = jnp.ones((16, 128), F32)
    scratch[:, 0:25] = light_ref[...]
    wide = scratch[...]
    inside = iota((16, 128), 1)
    scratch[...] = jnp.where((inside >= 32) & (inside < 57), pltpu.roll(wide, 32, axis=1), wide)
    for q in range(4):
        top = (q % 2) * 4
        light_out[q // 2, top : top + 4, :] = scratch[pl.ds(q, 4, stride=4), :]


def slopes_kernel(got_ref, light_ref, recon_ref, slopes_ref, out_ref, scratch):
    xl = lax.axis_index("xl")
    yh = lax.axis_index("yh")
    zl = lax.axis_index("zl")
    row = iota((8, 128), 0)
    lane = iota((8, 128), 1)
    mine = (row >> 2) == yh
    for source in range(16):
        block = got_ref[source]
        block = jnp.where(xl == 0, block, pltpu.roll(block, 64, axis=1))
        scratch[source] = jnp.where(mine, block, pltpu.roll(block, 4, axis=0))
    cell = lane & 31
    phases = [jnp.zeros((8, 128), F32), jnp.zeros((8, 128), F32)]
    flat_start = 100 * zl + 25 * ylc_index()
    for n in range(25):
        flat = flat_start + n
        lens_row = (flat * 205) >> 14
        lens_col = flat - 80 * lens_row
        kind = (lens_col * 205) >> 12
        index = lens_col - 20 * kind
        regular = index < 16
        source = jnp.where(regular, index, 4 * kind + index - 16)
        first = lens_row == zl + (kind < zl).astype(I32)
        place = jnp.where(regular, jnp.where(first, 4 * kind, 20), jnp.where(first, 16, 24))
        block = scratch[source]
        turned = [pltpu.roll(block, (n + 128 - q - place) & 127, axis=1) for q in range(4)]
        for h in range(2):
            pair = jnp.where(row < 4, turned[2 * h], turned[2 * h + 1])
            phases[h] = jnp.where(cell == n, pair, phases[h])
    re, im = [], []
    for h in range(2):
        light = light_ref[h]
        re.append(light * jnp.cos(phases[h]))
        im.append(light * jnp.sin(phases[h]))
    power = re[0] * re[0] + im[0] * im[0] + re[1] * re[1] + im[1] * im[1]
    flux = jnp.sum(power, axis=0, keepdims=True)
    along_p = -4.0 * power
    pixel = row & 3
    for h in range(2):
        for d in range(1, 4):
            back_re = pltpu.roll(re[h], d, axis=0)
            back_im = pltpu.roll(im[h], d, axis=0)
            same = re[h] * back_re + im[h] * back_im
            cross = im[h] * back_re - re[h] * back_im
            sign = -8.0 if d % 2 == 0 else 8.0
            term = sign * same + (4.0 * LAG[d - 1]) * cross
            along_p = along_p + jnp.where(pixel >= d, term, 0.0)
    swap_re = [pltpu.roll(x, 4, axis=0) for x in re]
    swap_im = [pltpu.roll(x, 4, axis=0) for x in im]

    def term_of(to_re, to_im, from_re, from_im, d):
        same = to_re * from_re + to_im * from_im
        cross = to_im * from_re - to_re * from_im
        sign = -8.0 if d % 2 == 0 else 8.0
        return sign * same + (4.0 * LAG[d - 1]) * cross

    along_q = -4.0 * power
    upper = row >= 4
    for h in range(2):
        along_q = along_q + jnp.where(upper, term_of(re[h], im[h], swap_re[h], swap_im[h], 1), 0.0)
    along_q = along_q + term_of(re[1], im[1], re[0], im[0], 2)
    near = term_of(re[1], im[1], swap_re[0], swap_im[0], 1)
    far = term_of(re[1], im[1], swap_re[0], swap_im[0], 3)
    along_q = along_q + jnp.where(upper, far, near)
    scale = 0.125 / flux
    slope_p = jnp.sum(along_p, axis=0, keepdims=True) * scale
    slope_q = jnp.sum(along_q, axis=0, keepdims=True) * scale
    pair = jnp.where(row == 0, slope_p, slope_q)
    compact = [pair, pltpu.roll(pair, 96, axis=1)]
    for frame in range(2):
        slopes_ref[frame] = compact[frame]
    total = jnp.zeros((8, ACTUATORS), F32)
    for axis in range(2):
        left = jnp.where(row == 0, compact[0][axis : axis + 1], compact[1][axis : axis + 1])
        left = left[:, 0:25].astype(BF16)
        total = total + jnp.dot(left, recon_ref[axis], preferred_element_type=F32)
    for j in range(23):
        out_ref[j] = total[0:2, 256 * j : 256 * j + 256]
    out_ref[23] = jnp.zeros((2, 256), F32)
    out_ref[23, :, 0:112] = total[0:2, 5888:6000]
    for j in range(24, 32):
        out_ref[j] = jnp.zeros((2, 256), F32)


def sum_kernel(got_ref, out_ref):
    total = jnp.sum(got_ref[...], axis=0)
    for i in range(out_ref.shape[0]):
        out_ref[i] = total


def clip_kernel(got_ref, code_ref, slopes_ref, slopes_out, out_ref):
    slopes_out[...] = slopes_ref[:, 0:2, 0:25]
    for j in range(24):
        width = 256 if j < 23 else 112
        update = got_ref[j][:, 0:width]
        limit = code_ref[256 * j : 256 * j + width].reshape(1, width).astype(F32) * 0.125
        first = jnp.clip(0.5 * update[0:1], -limit, limit)
        second = jnp.clip(first + 0.5 * update[1:2], -limit, limit)
        out_ref[0:1, 256 * j : 256 * j + width] = first
        out_ref[1:2, 256 * j : 256 * j + width] = second


def call(body, outs, specs, *args, scratch=(), name=None):
    return pl.pallas_call(
        body,
        out_shape=outs,
        in_specs=specs,
        out_specs=jax.tree.map(lambda _: VMEM, outs),
        scratch_shapes=list(scratch),
        compiler_params=pltpu.CompilerParams(vmem_limit_bytes=16 * 1024 * 1024),
        name=name,
    )(*args)


def exchange(value, axes):
    return lax.all_to_all(value, axes, 0, 0, tiled=True)


def shards(screens, row_offset, col_offset, layer_bin, illumination, reconstructor, sat_code):
    shape = jax.ShapeDtypeStruct
    row_offset = jnp.transpose(row_offset, (0, 2, 1))
    cols = call(columns_kernel, shape((32, 8, 128), F32), [SMEM, SMEM, VMEM], col_offset, layer_bin, screens, name="columns")
    cols = exchange(cols, PLANE)
    pupil, light = call(
        rows_kernel,
        (shape((16, 8, 128), F32), shape((2, 8, 128), F32)),
        [SMEM, SMEM, VMEM, VMEM],
        row_offset,
        layer_bin,
        illumination,
        cols,
        scratch=[pltpu.VMEM((16, 128), F32)],
        name="rows",
    )
    pupil = exchange(pupil, RING)
    owned = call(sum_kernel, shape((16, 8, 128), F32), [VMEM], pupil, name="spread")
    owned = exchange(owned, HALF)
    owned, reconstructor = lax.optimization_barrier((owned, reconstructor))
    slopes, updates = call(
        slopes_kernel,
        (shape((2, 8, 128), F32), shape((32, 2, 256), F32)),
        [VMEM, VMEM, VMEM],
        owned,
        light,
        reconstructor,
        scratch=[pltpu.VMEM((16, 8, 128), F32)],
        name="slopes",
    )
    updates = exchange(updates, PLANE)
    updates = call(sum_kernel, shape((16, 2, 256), F32), [VMEM], updates, name="sum_plane")
    updates = exchange(updates, RING)
    updates = call(sum_kernel, shape((32, 2, 256), F32), [VMEM], updates, name="sum_ring")
    updates = exchange(updates, PLANE)
    return call(
        clip_kernel,
        (shape((2, 2, 25), F32), shape((2, ACTUATORS), F32)),
        [VMEM, VMEM, VMEM],
        updates,
        sat_code,
        slopes,
        name="clip",
    )


def solution(mesh):
    fine = Mesh(mesh.devices.reshape(SIZES), NAMES)
    placed = (
        P(ALT, STRIP, None),
        P(),
        P(),
        P(),
        P(None, ALT + STRIP),
        P(None, ALT + STRIP, None),
        P(),
    )
    return jax.shard_map(
        shards,
        mesh=fine,
        in_specs=placed,
        out_specs=(P(None, None, ALT + STRIP), P()),
        check_vma=False,
    )
```

```python
import jax
import jax.numpy as jnp
from jax import lax
from jax.experimental import pallas as pl
from jax.experimental.pallas import tpu as pltpu
from jax.sharding import Mesh, PartitionSpec as P

ACTUATORS = 6000
F32 = jnp.float32
BF16 = jnp.bfloat16
I32 = jnp.int32

NAMES = ("xh", "xl", "yh", "zh", "zl", "yl", "co")
SIZES = (2, 2, 2, 4, 4, 2, 2)
ALT = ("xh", "xl", "yh")
STRIP = ("zh", "zl", "yl", "co")
PLANE = ("xh", "xl", "yh", "yl", "co")
HALF = ("xl", "yh", "yl", "co")
RING = ("zh", "zl")

ROOT = 2.0**0.5
LAG = (2.0 + 2.0 * ROOT, -2.0, 2.0 * ROOT - 2.0)

VMEM = pl.BlockSpec(memory_space=pltpu.VMEM)


def iota(shape, dim):
    return lax.broadcasted_iota(I32, shape, dim)


def alt_index():
    return lax.axis_index("xh") * 4 + lax.axis_index("xl") * 2 + lax.axis_index("yh")


def ylc_index():
    return lax.axis_index("yl") * 2 + lax.axis_index("co")


def block_index():
    return (lax.axis_index("xl") * 2 + lax.axis_index("yh")) * 4 + ylc_index()


def columns_kernel(col_ref, bin_ref, screen_ref, out_ref):
    alt = alt_index()
    lane = iota((1, 512), 1)
    block = lane >> 5
    part = (lane & 31) >> 2
    lenslet = jnp.where(part < 4, 20 * part + block, 20 * (block >> 2) + 16 + (block & 3))
    column = (4 * lenslet + (lane & 3)).astype(F32)
    position = iota((384, 512), 0).astype(F32)
    results = []
    bins = bin_ref[...].reshape(1, 16)
    lefts = [col_ref[frame, pl.ds(2 * alt, 2), :] for frame in range(2)]
    for layer in range(2):
        chosen = jnp.where(iota((1, 16), 1) == 2 * alt + layer, bins, 0).astype(F32)
        shrink = 1.0 - jnp.sum(chosen, axis=1, keepdims=True) * 0.03125
        weights = jnp.maximum(0.0, 1.0 - jnp.abs(position - column * shrink)).astype(BF16)
        rows = screen_ref[layer].astype(F32)
        parts = []
        for frame in range(2):
            for star in range(2):
                turned = pltpu.roll(rows, (512 - lefts[frame][layer, star]) & 511, axis=1)
                parts.append(turned[:, :384])
        stacked = jnp.concatenate(parts, axis=0).astype(BF16)
        results.append(jnp.dot(stacked, weights, preferred_element_type=F32))
    group = iota((8, 128), 1) >> 5
    for star in range(2):
        for tile in range(4):
            slots = []
            for layer in range(2):
                for frame in range(2):
                    top = (frame * 2 + star) * 8
                    slots.append(results[layer][top : top + 8, tile * 128 : tile * 128 + 128])
            for inner in range(4):
                merged = jnp.zeros((8, 128), F32)
                for slot in range(4):
                    shift = (32 * (slot - inner)) % 128
                    moved = slots[slot] if shift == 0 else pltpu.roll(slots[slot], shift, axis=1)
                    merged = jnp.where(group == slot, moved, merged)
                out_ref[star * 16 + tile * 4 + inner] = merged


def rows_kernel(row_ref, bin_ref, light_ref, got_ref, out_ref, light_out, scratch):
    star = lax.axis_index("xh")
    block = block_index()
    ring = lax.axis_index("zh") * 4 + lax.axis_index("zl")
    values = got_ref[...].reshape(256, 128)
    high = values.astype(BF16).astype(F32)
    low = values - high
    wide = iota((256, 128), 1)
    rights = [
        jnp.where(wide < 64, high, pltpu.roll(low, 64, axis=1)).astype(BF16),
        jnp.where(wide < 64, pltpu.roll(high, 64, axis=1), low).astype(BF16),
    ]
    line = iota((64, 1), 0)
    base = (80 * ((line >> 2) & 3) + 20 * (line >> 4) + (line & 3)).astype(F32)
    pupil_row = jnp.concatenate([base + 4.0 * rr for rr in range(5)], axis=0)
    screen_row = (ring * 32 + (iota((1, 256), 1) & 31)).astype(F32)
    tops = [jnp.where(star == 0, row_ref[frame, 0:1, :], row_ref[frame, 1:2, :]) for frame in range(2)]
    parts = [top >> 4 for top in tops] + [top & 15 for top in tops] + [bin_ref[...].reshape(1, 16)]
    line16 = iota((8, 16), 0)
    packed = jnp.zeros((8, 16), F32)
    for n, part in enumerate(parts):
        packed = jnp.where(line16 == n, part.astype(F32), packed)
    packed = packed.astype(BF16)
    sums = [None, None]
    for layer in range(2):
        pick = (iota((16, 256), 0) == 2 * (iota((16, 256), 1) >> 5) + layer).astype(F32).astype(BF16)
        lanes = jnp.dot(packed, pick, preferred_element_type=F32)
        scaled = pupil_row * (1.0 - lanes[4:5] * 0.03125)
        for frame in range(2):
            offset = screen_row - (16.0 * lanes[frame : frame + 1] + lanes[2 + frame : 3 + frame])
            weights = jnp.maximum(0.0, 1.0 - jnp.abs(offset - scaled)).astype(BF16)
            term = jnp.dot(weights, rights[layer], preferred_element_type=F32)
            sums[frame] = term if layer == 0 else sums[frame] + term
    lane = iota((8, 128), 1)
    cell = lane & 31
    odd = (lane & 32) != 0
    kind = jnp.where(cell < 16, cell >> 2, block >> 2)
    for t in range(4):
        pieces = []
        for rr in range(5):
            halves = []
            for h in range(2):
                start = rr * 64 + t * 16 + h * 8
                both = jnp.where(odd, sums[1][start : start + 8], sums[0][start : start + 8])
                halves.append(both + pltpu.roll(both, 64, axis=1))
            pieces.append(jnp.where(lane < 64, halves[0], halves[1]))
        for zl in range(4):
            here, after = pieces[zl], pieces[zl + 1]
            first = jnp.where(kind < zl, after, here)
            second = jnp.where(cell < 24, pltpu.roll(after, 20 - 4 * zl, axis=1), pltpu.roll(after, 8, axis=1))
            out_ref[t * 4 + zl] = jnp.where(cell < 20, first, second)
    scratch[...] = jnp.ones((16, 128), F32)
    scratch[:, 0:25] = light_ref[...]
    wide = scratch[...]
    inside = iota((16, 128), 1)
    scratch[...] = jnp.where((inside >= 32) & (inside < 57), pltpu.roll(wide, 32, axis=1), wide)
    for q in range(4):
        top = (q % 2) * 4
        light_out[q // 2, top : top + 4, :] = scratch[pl.ds(q, 4, stride=4), :]


def spread_kernel(got_ref, out_ref):
    total = jnp.sum(got_ref[...], axis=0)
    turned = [total, pltpu.roll(total, 64, axis=1)]
    for quarter in range(4):
        piece = turned[quarter // 2][(quarter % 2) * 4 : (quarter % 2) * 4 + 4]
        for ylc in range(4):
            out_ref[quarter * 4 + ylc] = piece


def slopes_kernel(got_ref, light_ref, recon_ref, slopes_ref, out_ref):
    zl = lax.axis_index("zl")
    row = iota((8, 128), 0)
    lane = iota((8, 128), 1)
    cell = lane & 31
    phases = [jnp.zeros((8, 128), F32), jnp.zeros((8, 128), F32)]
    flat_start = 100 * zl + 25 * ylc_index()
    for n in range(25):
        flat = flat_start + n
        lens_row = (flat * 205) >> 14
        lens_col = flat - 80 * lens_row
        kind = (lens_col * 205) >> 12
        index = lens_col - 20 * kind
        regular = index < 16
        source = jnp.where(regular, index, 4 * kind + index - 16)
        first = lens_row == zl + (kind < zl).astype(I32)
        place = jnp.where(regular, jnp.where(first, 4 * kind, 20), jnp.where(first, 16, 24))
        block = got_ref[source]
        block = jnp.concatenate([block, block], axis=0)
        turned = [pltpu.roll(block, (n + 128 - q - place) & 127, axis=1) for q in range(4)]
        for h in range(2):
            pair = jnp.where(row < 4, turned[2 * h], turned[2 * h + 1])
            phases[h] = jnp.where(cell == n, pair, phases[h])
    re, im = [], []
    for h in range(2):
        light = light_ref[h]
        re.append(light * jnp.cos(phases[h]))
        im.append(light * jnp.sin(phases[h]))
    power = re[0] * re[0] + im[0] * im[0] + re[1] * re[1] + im[1] * im[1]
    flux = jnp.sum(power, axis=0, keepdims=True)
    along_p = -4.0 * power
    pixel = row & 3
    for h in range(2):
        for d in range(1, 4):
            back_re = pltpu.roll(re[h], d, axis=0)
            back_im = pltpu.roll(im[h], d, axis=0)
            same = re[h] * back_re + im[h] * back_im
            cross = im[h] * back_re - re[h] * back_im
            sign = -8.0 if d % 2 == 0 else 8.0
            term = sign * same + (4.0 * LAG[d - 1]) * cross
            along_p = along_p + jnp.where(pixel >= d, term, 0.0)
    swap_re = [pltpu.roll(x, 4, axis=0) for x in re]
    swap_im = [pltpu.roll(x, 4, axis=0) for x in im]

    def term_of(to_re, to_im, from_re, from_im, d):
        same = to_re * from_re + to_im * from_im
        cross = to_im * from_re - to_re * from_im
        sign = -8.0 if d % 2 == 0 else 8.0
        return sign * same + (4.0 * LAG[d - 1]) * cross

    along_q = -4.0 * power
    upper = row >= 4
    for h in range(2):
        along_q = along_q + jnp.where(upper, term_of(re[h], im[h], swap_re[h], swap_im[h], 1), 0.0)
    along_q = along_q + term_of(re[1], im[1], re[0], im[0], 2)
    near = term_of(re[1], im[1], swap_re[0], swap_im[0], 1)
    far = term_of(re[1], im[1], swap_re[0], swap_im[0], 3)
    along_q = along_q + jnp.where(upper, far, near)
    scale = 0.125 / flux
    slope_p = jnp.sum(along_p, axis=0, keepdims=True) * scale
    slope_q = jnp.sum(along_q, axis=0, keepdims=True) * scale
    pair = jnp.where(row == 0, slope_p, slope_q)
    compact = [pair, pltpu.roll(pair, 96, axis=1)]
    for frame in range(2):
        slopes_ref[frame] = compact[frame]
    total = jnp.zeros((8, ACTUATORS), F32)
    for axis in range(2):
        left = jnp.where(row == 0, compact[0][axis : axis + 1], compact[1][axis : axis + 1])
        left = left[:, 0:25].astype(BF16)
        total = total + jnp.dot(left, recon_ref[axis], preferred_element_type=F32)
    for j in range(23):
        out_ref[j] = total[0:2, 256 * j : 256 * j + 256]
    out_ref[23] = jnp.zeros((2, 256), F32)
    out_ref[23, :, 0:112] = total[0:2, 5888:6000]
    for j in range(24, 32):
        out_ref[j] = jnp.zeros((2, 256), F32)


def sum_kernel(got_ref, out_ref):
    total = jnp.sum(got_ref[...], axis=0)
    for i in range(out_ref.shape[0]):
        out_ref[i] = total


def clip_kernel(got_ref, code_ref, slopes_ref, slopes_out, out_ref):
    slopes_out[...] = slopes_ref[:, 0:2, 0:25]
    for j in range(24):
        width = 256 if j < 23 else 112
        update = got_ref[j][:, 0:width]
        limit = code_ref[256 * j : 256 * j + width].reshape(1, width).astype(F32) * 0.125
        first = jnp.clip(0.5 * update[0:1], -limit, limit)
        second = jnp.clip(first + 0.5 * update[1:2], -limit, limit)
        out_ref[0:1, 256 * j : 256 * j + width] = first
        out_ref[1:2, 256 * j : 256 * j + width] = second


def call(body, outs, specs, *args, scratch=(), name=None):
    return pl.pallas_call(
        body,
        out_shape=outs,
        in_specs=specs,
        out_specs=jax.tree.map(lambda _: VMEM, outs),
        scratch_shapes=list(scratch),
        compiler_params=pltpu.CompilerParams(vmem_limit_bytes=16 * 1024 * 1024),
        name=name,
    )(*args)


def exchange(value, axes):
    return lax.all_to_all(value, axes, 0, 0, tiled=True)


def shards(screens, row_offset, col_offset, layer_bin, illumination, reconstructor, sat_code):
    shape = jax.ShapeDtypeStruct
    row_offset = jnp.transpose(row_offset, (0, 2, 1))
    cols = call(columns_kernel, shape((32, 8, 128), F32), [VMEM, VMEM, VMEM], col_offset, layer_bin, screens, name="columns")
    cols = exchange(cols, PLANE)
    pupil, light = call(
        rows_kernel,
        (shape((16, 8, 128), F32), shape((2, 8, 128), F32)),
        [VMEM, VMEM, VMEM, VMEM],
        row_offset,
        layer_bin,
        illumination,
        cols,
        scratch=[pltpu.VMEM((16, 128), F32)],
        name="rows",
    )
    pupil = exchange(pupil, RING)
    owned = call(spread_kernel, shape((16, 4, 128), F32), [VMEM], pupil, name="spread")
    owned = exchange(owned, HALF)
    owned, reconstructor = lax.optimization_barrier((owned, reconstructor))
    slopes, updates = call(
        slopes_kernel,
        (shape((2, 8, 128), F32), shape((32, 2, 256), F32)),
        [VMEM, VMEM, VMEM],
        owned,
        light,
        reconstructor,
        name="slopes",
    )
    updates = exchange(updates, PLANE)
    updates = call(sum_kernel, shape((16, 2, 256), F32), [VMEM], updates, name="sum_plane")
    updates = exchange(updates, RING)
    updates = call(sum_kernel, shape((32, 2, 256), F32), [VMEM], updates, name="sum_ring")
    updates = exchange(updates, PLANE)
    return call(
        clip_kernel,
        (shape((2, 2, 25), F32), shape((2, ACTUATORS), F32)),
        [VMEM, VMEM, VMEM],
        updates,
        sat_code,
        slopes,
        name="clip",
    )


def solution(mesh):
    fine = Mesh(mesh.devices.reshape(SIZES), NAMES)
    placed = (
        P(ALT, STRIP, None),
        P(),
        P(),
        P(),
        P(None, ALT + STRIP),
        P(None, ALT + STRIP, None),
        P(),
    )
    return jax.shard_map(
        shards,
        mesh=fine,
        in_specs=placed,
        out_specs=(P(None, None, ALT + STRIP), P()),
        check_vma=False,
    )
```

```python
import jax
import jax.numpy as jnp
from jax import lax
from jax.experimental import pallas as pl
from jax.experimental.pallas import tpu as pltpu
from jax.sharding import Mesh, PartitionSpec as P

ACTUATORS = 6000
F32 = jnp.float32
BF16 = jnp.bfloat16
I32 = jnp.int32

NAMES = ("xh", "xl", "yh", "zh", "zl", "yl", "co")
SIZES = (2, 2, 2, 4, 4, 2, 2)
ALT = ("xh", "xl", "yh")
STRIP = ("zh", "zl", "yl", "co")
PLANE = ("xh", "xl", "yh", "yl", "co")
HALF = ("xl", "yh", "yl", "co")
RING = ("zh", "zl")

ROOT = 2.0**0.5
LAG = (2.0 + 2.0 * ROOT, -2.0, 2.0 * ROOT - 2.0)

VMEM = pl.BlockSpec(memory_space=pltpu.VMEM)


def iota(shape, dim):
    return lax.broadcasted_iota(I32, shape, dim)


def alt_index():
    return lax.axis_index("xh") * 4 + lax.axis_index("xl") * 2 + lax.axis_index("yh")


def ylc_index():
    return lax.axis_index("yl") * 2 + lax.axis_index("co")


def block_index():
    return (lax.axis_index("xl") * 2 + lax.axis_index("yh")) * 4 + ylc_index()


def columns_kernel(col_ref, bin_ref, screen_ref, out_ref):
    alt = alt_index()
    lane = iota((1, 512), 1)
    block = lane >> 5
    part = (lane & 31) >> 2
    lenslet = jnp.where(part < 4, 20 * part + block, 20 * (block >> 2) + 16 + (block & 3))
    column = (4 * lenslet + (lane & 3)).astype(F32)
    position = iota((384, 512), 0).astype(F32)
    results = []
    bins = bin_ref[...].reshape(1, 16)
    lefts = [col_ref[frame, pl.ds(2 * alt, 2), :] for frame in range(2)]
    for layer in range(2):
        chosen = jnp.where(iota((1, 16), 1) == 2 * alt + layer, bins, 0).astype(F32)
        shrink = 1.0 - jnp.sum(chosen, axis=1, keepdims=True) * 0.03125
        weights = jnp.maximum(0.0, 1.0 - jnp.abs(position - column * shrink)).astype(BF16)
        rows = screen_ref[layer].astype(F32)
        parts = []
        for frame in range(2):
            for star in range(2):
                turned = pltpu.roll(rows, (512 - lefts[frame][layer, star]) & 511, axis=1)
                parts.append(turned[:, :384])
        stacked = jnp.concatenate(parts, axis=0).astype(BF16)
        results.append(jnp.dot(stacked, weights, preferred_element_type=F32))
    group = iota((8, 128), 1) >> 5
    for star in range(2):
        for tile in range(4):
            slots = []
            for layer in range(2):
                for frame in range(2):
                    top = (frame * 2 + star) * 8
                    slots.append(results[layer][top : top + 8, tile * 128 : tile * 128 + 128])
            for inner in range(4):
                merged = jnp.zeros((8, 128), F32)
                for slot in range(4):
                    shift = (32 * (slot - inner)) % 128
                    moved = slots[slot] if shift == 0 else pltpu.roll(slots[slot], shift, axis=1)
                    merged = jnp.where(group == slot, moved, merged)
                out_ref[star * 16 + tile * 4 + inner] = merged


def rows_kernel(row_ref, bin_ref, light_ref, got_ref, out_ref, light_out, scratch):
    star = lax.axis_index("xh")
    block = block_index()
    ring = lax.axis_index("zh") * 4 + lax.axis_index("zl")
    values = got_ref[...].reshape(256, 128)
    high = values.astype(BF16).astype(F32)
    low = values - high
    wide = iota((256, 128), 1)
    rights = [
        jnp.where(wide < 64, high, pltpu.roll(low, 64, axis=1)).astype(BF16),
        jnp.where(wide < 64, pltpu.roll(high, 64, axis=1), low).astype(BF16),
    ]
    line = iota((64, 1), 0)
    base = (80 * ((line >> 2) & 3) + 20 * (line >> 4) + (line & 3)).astype(F32)
    pupil_row = jnp.concatenate([base + 4.0 * rr for rr in range(5)], axis=0)
    screen_row = (ring * 32 + (iota((1, 256), 1) & 31)).astype(F32)
    tops = [jnp.where(star == 0, row_ref[frame, 0:1, :], row_ref[frame, 1:2, :]) for frame in range(2)]
    parts = [top >> 4 for top in tops] + [top & 15 for top in tops] + [bin_ref[...].reshape(1, 16)]
    line16 = iota((8, 16), 0)
    packed = jnp.zeros((8, 16), F32)
    for n, part in enumerate(parts):
        packed = jnp.where(line16 == n, part.astype(F32), packed)
    packed = packed.astype(BF16)
    sums = [None, None]
    for layer in range(2):
        pick = (iota((16, 256), 0) == 2 * (iota((16, 256), 1) >> 5) + layer).astype(F32).astype(BF16)
        lanes = jnp.dot(packed, pick, preferred_element_type=F32)
        scaled = pupil_row * (1.0 - lanes[4:5] * 0.03125)
        for frame in range(2):
            offset = screen_row - (16.0 * lanes[frame : frame + 1] + lanes[2 + frame : 3 + frame])
            weights = jnp.maximum(0.0, 1.0 - jnp.abs(offset - scaled)).astype(BF16)
            term = jnp.dot(weights, rights[layer], preferred_element_type=F32)
            sums[frame] = term if layer == 0 else sums[frame] + term
    lane = iota((8, 128), 1)
    cell = lane & 31
    odd = (lane & 32) != 0
    kind = jnp.where(cell < 16, cell >> 2, block >> 2)
    for t in range(4):
        pieces = []
        for rr in range(5):
            halves = []
            for h in range(2):
                start = rr * 64 + t * 16 + h * 8
                both = jnp.where(odd, sums[1][start : start + 8], sums[0][start : start + 8])
                halves.append(both + pltpu.roll(both, 64, axis=1))
            pieces.append(jnp.where(lane < 64, halves[0], halves[1]))
        for zl in range(4):
            here, after = pieces[zl], pieces[zl + 1]
            first = jnp.where(kind < zl, after, here)
            second = jnp.where(cell < 24, pltpu.roll(after, 20 - 4 * zl, axis=1), pltpu.roll(after, 8, axis=1))
            out_ref[t * 4 + zl] = jnp.where(cell < 20, first, second)
    scratch[...] = jnp.ones((16, 128), F32)
    scratch[:, 0:25] = light_ref[...]
    wide = scratch[...]
    inside = iota((16, 128), 1)
    scratch[...] = jnp.where((inside >= 32) & (inside < 57), pltpu.roll(wide, 32, axis=1), wide)
    for q in range(4):
        top = (q % 2) * 4
        light_out[q // 2, top : top + 4, :] = scratch[pl.ds(q, 4, stride=4), :]


def spread_kernel(got_ref, out_ref):
    total = jnp.sum(got_ref[...], axis=0)
    turned = [total, pltpu.roll(total, 64, axis=1)]
    for quarter in range(4):
        piece = turned[quarter // 2][(quarter % 2) * 4 : (quarter % 2) * 4 + 4]
        for ylc in range(4):
            out_ref[quarter * 4 + ylc] = piece


def slopes_kernel(got_ref, light_ref, recon_ref, slopes_ref, out_ref):
    zl = lax.axis_index("zl")
    row = iota((8, 128), 0)
    lane = iota((8, 128), 1)
    cell = lane & 31
    phases = [jnp.zeros((8, 128), F32), jnp.zeros((8, 128), F32)]
    flat_start = 100 * zl + 25 * ylc_index()
    for n in range(25):
        flat = flat_start + n
        lens_row = (flat * 205) >> 14
        lens_col = flat - 80 * lens_row
        kind = (lens_col * 205) >> 12
        index = lens_col - 20 * kind
        regular = index < 16
        source = jnp.where(regular, index, 4 * kind + index - 16)
        first = lens_row == zl + (kind < zl).astype(I32)
        place = jnp.where(regular, jnp.where(first, 4 * kind, 20), jnp.where(first, 16, 24))
        block = got_ref[source]
        block = jnp.concatenate([block, block], axis=0)
        turned = [pltpu.roll(block, (n + 128 - q - place) & 127, axis=1) for q in range(4)]
        for h in range(2):
            pair = jnp.where(row < 4, turned[2 * h], turned[2 * h + 1])
            phases[h] = jnp.where(cell == n, pair, phases[h])
    re, im = [], []
    for h in range(2):
        light = light_ref[h]
        re.append(light * jnp.cos(phases[h]))
        im.append(light * jnp.sin(phases[h]))
    power = re[0] * re[0] + im[0] * im[0] + re[1] * re[1] + im[1] * im[1]
    flux = jnp.sum(power, axis=0, keepdims=True)
    along_p = -4.0 * power
    pixel = row & 3
    for h in range(2):
        for d in range(1, 4):
            back_re = pltpu.roll(re[h], d, axis=0)
            back_im = pltpu.roll(im[h], d, axis=0)
            same = re[h] * back_re + im[h] * back_im
            cross = im[h] * back_re - re[h] * back_im
            sign = -8.0 if d % 2 == 0 else 8.0
            term = sign * same + (4.0 * LAG[d - 1]) * cross
            along_p = along_p + jnp.where(pixel >= d, term, 0.0)
    swap_re = [pltpu.roll(x, 4, axis=0) for x in re]
    swap_im = [pltpu.roll(x, 4, axis=0) for x in im]

    def term_of(to_re, to_im, from_re, from_im, d):
        same = to_re * from_re + to_im * from_im
        cross = to_im * from_re - to_re * from_im
        sign = -8.0 if d % 2 == 0 else 8.0
        return sign * same + (4.0 * LAG[d - 1]) * cross

    along_q = -4.0 * power
    upper = row >= 4
    for h in range(2):
        along_q = along_q + jnp.where(upper, term_of(re[h], im[h], swap_re[h], swap_im[h], 1), 0.0)
    along_q = along_q + term_of(re[1], im[1], re[0], im[0], 2)
    near = term_of(re[1], im[1], swap_re[0], swap_im[0], 1)
    far = term_of(re[1], im[1], swap_re[0], swap_im[0], 3)
    along_q = along_q + jnp.where(upper, far, near)
    scale = 0.125 / flux
    slope_p = jnp.sum(along_p, axis=0, keepdims=True) * scale
    slope_q = jnp.sum(along_q, axis=0, keepdims=True) * scale
    pair = jnp.where(row == 0, slope_p, slope_q)
    compact = [pair, pltpu.roll(pair, 96, axis=1)]
    for frame in range(2):
        slopes_ref[frame] = compact[frame]
    total = jnp.zeros((8, ACTUATORS), F32)
    for axis in range(2):
        left = jnp.where(row == 0, compact[0][axis : axis + 1], compact[1][axis : axis + 1])
        left = left[:, 0:25].astype(BF16)
        total = total + jnp.dot(left, recon_ref[axis], preferred_element_type=F32)
    for j in range(32):
        start = 384 * (j % 16)
        width = min(384, ACTUATORS - start)
        if width < 384:
            out_ref[j] = jnp.zeros((1, 384), F32)
        out_ref[j, :, 0:width] = total[j // 16 : j // 16 + 1, start : start + width]


def sum_kernel(got_ref, out_ref):
    total = jnp.sum(got_ref[...], axis=0)
    for i in range(out_ref.shape[0]):
        out_ref[i] = total


def clip_kernel(got_ref, code_ref, slopes_ref, slopes_out, out_ref):
    slopes_out[...] = slopes_ref[:, 0:2, 0:25]
    for j in range(16):
        start = 384 * j
        width = min(384, ACTUATORS - start)
        limit = code_ref[start : start + width].reshape(1, width).astype(F32) * 0.125
        first = jnp.clip(0.5 * got_ref[j][:, 0:width], -limit, limit)
        second = jnp.clip(first + 0.5 * got_ref[16 + j][:, 0:width], -limit, limit)
        out_ref[0:1, start : start + width] = first
        out_ref[1:2, start : start + width] = second


def call(body, outs, specs, *args, scratch=(), name=None):
    return pl.pallas_call(
        body,
        out_shape=outs,
        in_specs=specs,
        out_specs=jax.tree.map(lambda _: VMEM, outs),
        scratch_shapes=list(scratch),
        compiler_params=pltpu.CompilerParams(vmem_limit_bytes=16 * 1024 * 1024),
        name=name,
    )(*args)


def exchange(value, axes):
    return lax.all_to_all(value, axes, 0, 0, tiled=True)


def shards(screens, row_offset, col_offset, layer_bin, illumination, reconstructor, sat_code):
    shape = jax.ShapeDtypeStruct
    row_offset = jnp.transpose(row_offset, (0, 2, 1))
    cols = call(columns_kernel, shape((32, 8, 128), F32), [VMEM, VMEM, VMEM], col_offset, layer_bin, screens, name="columns")
    cols = exchange(cols, PLANE)
    pupil, light = call(
        rows_kernel,
        (shape((16, 8, 128), F32), shape((2, 8, 128), F32)),
        [VMEM, VMEM, VMEM, VMEM],
        row_offset,
        layer_bin,
        illumination,
        cols,
        scratch=[pltpu.VMEM((16, 128), F32)],
        name="rows",
    )
    pupil = exchange(pupil, RING)
    owned = call(spread_kernel, shape((16, 4, 128), F32), [VMEM], pupil, name="spread")
    owned = exchange(owned, HALF)
    owned, reconstructor = lax.optimization_barrier((owned, reconstructor))
    slopes, updates = call(
        slopes_kernel,
        (shape((2, 8, 128), F32), shape((32, 1, 384), F32)),
        [VMEM, VMEM, VMEM],
        owned,
        light,
        reconstructor,
        name="slopes",
    )
    updates = exchange(updates, PLANE)
    updates = call(sum_kernel, shape((16, 1, 384), F32), [VMEM], updates, name="sum_plane")
    updates = exchange(updates, RING)
    updates = call(sum_kernel, shape((32, 1, 384), F32), [VMEM], updates, name="sum_ring")
    updates = exchange(updates, PLANE)
    return call(
        clip_kernel,
        (shape((2, 2, 25), F32), shape((2, ACTUATORS), F32)),
        [VMEM, VMEM, VMEM],
        updates,
        sat_code,
        slopes,
        name="clip",
    )


def solution(mesh):
    fine = Mesh(mesh.devices.reshape(SIZES), NAMES)
    placed = (
        P(ALT, STRIP, None),
        P(),
        P(),
        P(),
        P(None, ALT + STRIP),
        P(None, ALT + STRIP, None),
        P(),
    )
    return jax.shard_map(
        shards,
        mesh=fine,
        in_specs=placed,
        out_specs=(P(None, None, ALT + STRIP), P()),
        check_vma=False,
    )
```

```python
import jax
import jax.numpy as jnp
from jax import lax
from jax.experimental import pallas as pl
from jax.experimental.pallas import tpu as pltpu
from jax.sharding import Mesh, PartitionSpec as P

ACTUATORS = 6000
F32 = jnp.float32
BF16 = jnp.bfloat16
I32 = jnp.int32

NAMES = ("xh", "xl", "yh", "zh", "zl", "yl", "co")
SIZES = (2, 2, 2, 4, 4, 2, 2)
ALT = ("xh", "xl", "yh")
STRIP = ("zh", "zl", "yl", "co")
PLANE = ("xh", "xl", "yh", "yl", "co")
EIGHT = ("xl", "yl", "co")
RING = ("zh", "zl")

ROOT = 2.0**0.5
LAG = (2.0 + 2.0 * ROOT, -2.0, 2.0 * ROOT - 2.0)

VMEM = pl.BlockSpec(memory_space=pltpu.VMEM)


def iota(shape, dim):
    return lax.broadcasted_iota(I32, shape, dim)


def alt_index():
    return lax.axis_index("xh") * 4 + lax.axis_index("xl") * 2 + lax.axis_index("yh")


def ylc_index():
    return lax.axis_index("yl") * 2 + lax.axis_index("co")


def block_index():
    return lax.axis_index("xl") * 4 + ylc_index()


def columns_kernel(col_ref, bin_ref, screen_ref, out_ref):
    alt = alt_index()
    lane = iota((1, 512), 1)
    block = lane >> 6
    part = (lane & 63) >> 2
    more = 20 * (block >> 1) + 16 + 2 * (block & 1)
    lenslet = jnp.where(part < 8, 20 * (part >> 1) + 2 * block, more) + (part & 1)
    column = (4 * lenslet + (lane & 3)).astype(F32)
    position = iota((384, 512), 0).astype(F32)
    results = []
    bins = bin_ref[...].reshape(1, 16)
    lefts = [col_ref[frame, pl.ds(2 * alt, 2), :] for frame in range(2)]
    for layer in range(2):
        chosen = jnp.where(iota((1, 16), 1) == 2 * alt + layer, bins, 0).astype(F32)
        shrink = 1.0 - jnp.sum(chosen, axis=1, keepdims=True) * 0.03125
        weights = jnp.maximum(0.0, 1.0 - jnp.abs(position - column * shrink)).astype(BF16)
        rows = screen_ref[layer].astype(F32)
        parts = []
        for frame in range(2):
            for star in range(2):
                turned = pltpu.roll(rows, (512 - lefts[frame][layer, star]) & 511, axis=1)
                parts.append(turned[:, :384])
        stacked = jnp.concatenate(parts, axis=0).astype(BF16)
        results.append(jnp.dot(stacked, weights, preferred_element_type=F32))
    left_half = iota((8, 128), 1) < 64
    for star in range(2):
        for block in range(8):
            start = (block // 2) * 128
            for layer in range(2):
                zero = results[layer][star * 8 : star * 8 + 8, start : start + 128]
                one = results[layer][16 + star * 8 : 24 + star * 8, start : start + 128]
                if block % 2 == 0:
                    one = pltpu.roll(one, 64, axis=1)
                else:
                    zero = pltpu.roll(zero, 64, axis=1)
                merged = jnp.where(left_half, zero, one)
                for yh in range(2):
                    to = star * 16 + (block // 4) * 8 + yh * 4 + block % 4
                    out_ref[to, :, layer * 128 : layer * 128 + 128] = merged


def rows_kernel(row_ref, bin_ref, light_ref, got_ref, out_ref, light_out, scratch):
    star = lax.axis_index("xh")
    block = block_index()
    ring = lax.axis_index("zh") * 4 + lax.axis_index("zl")
    values = got_ref[...].reshape(256, 256)
    high = values.astype(BF16)
    low = (values - high.astype(F32)).astype(BF16)
    rights = [
        jnp.concatenate([high[:, at : at + 128], low[:, at : at + 128]], axis=1) for at in (0, 128)
    ]
    line = iota((32, 1), 0)
    quarter = 2 * ((line >> 2) & 1) + lax.axis_index("yh")
    base = (80 * quarter + 20 * (line >> 3) + (line & 3)).astype(F32)
    pupil_row = jnp.concatenate([base + 4.0 * rr for rr in range(5)], axis=0)
    screen_row = (ring * 32 + (iota((1, 256), 1) & 31)).astype(F32)
    tops = [jnp.where(star == 0, row_ref[frame, 0:1, :], row_ref[frame, 1:2, :]) for frame in range(2)]
    parts = [top >> 4 for top in tops] + [top & 15 for top in tops] + [bin_ref[...].reshape(1, 16)]
    line16 = iota((8, 16), 0)
    packed = jnp.zeros((8, 16), F32)
    for n, part in enumerate(parts):
        packed = jnp.where(line16 == n, part.astype(F32), packed)
    packed = packed.astype(BF16)
    sums = [None, None]
    for layer in range(2):
        pick = (iota((16, 256), 0) == 2 * (iota((16, 256), 1) >> 5) + layer).astype(F32).astype(BF16)
        lanes = jnp.dot(packed, pick, preferred_element_type=F32)
        scaled = pupil_row * (1.0 - lanes[4:5] * 0.03125)
        for frame in range(2):
            offset = screen_row - (16.0 * lanes[frame : frame + 1] + lanes[2 + frame : 3 + frame])
            weights = jnp.maximum(0.0, 1.0 - jnp.abs(offset - scaled)).astype(BF16)
            term = jnp.dot(weights, rights[layer], preferred_element_type=F32)
            sums[frame] = term if layer == 0 else sums[frame] + term
    sums = [total[:, :128] + total[:, 128:] for total in sums]
    merged = jnp.where(iota((160, 128), 1) < 64, sums[0], sums[1])
    cell = iota((8, 128), 1) & 63
    kind = jnp.where(cell < 32, cell >> 3, block >> 1)
    for t in range(4):
        pieces = [merged[rr * 32 + t * 8 : rr * 32 + t * 8 + 8] for rr in range(5)]
        for zl in range(4):
            here, after = pieces[zl], pieces[zl + 1]
            first = jnp.where(kind < zl, after, here)
            second = jnp.where(cell < 48, pltpu.roll(after, 40 - 8 * zl, axis=1), pltpu.roll(after, 16, axis=1))
            out_ref[t * 4 + zl] = jnp.where(cell < 40, first, second)
    scratch[...] = jnp.ones((16, 128), F32)
    scratch[:, 0:25] = light_ref[...]
    wide = scratch[...]
    inside = iota((16, 128), 1)
    scratch[...] = jnp.where((inside >= 64) & (inside < 89), pltpu.roll(wide, 64, axis=1), wide)
    for q in range(4):
        top = (q % 2) * 4
        light_out[q // 2, top : top + 4, :] = scratch[pl.ds(q, 4, stride=4), :]


def spread_kernel(got_ref, out_ref):
    total = jnp.sum(got_ref[...], axis=0)
    for to in range(8):
        top = (to // 4) * 4
        out_ref[to] = total[top : top + 4]


def slopes_kernel(got_ref, light_ref, recon_ref, slopes_ref, out_ref):
    zl = lax.axis_index("zl")
    row = iota((8, 128), 0)
    lane = iota((8, 128), 1)
    cell = lane & 63
    phases = [jnp.zeros((8, 128), F32), jnp.zeros((8, 128), F32)]
    flat_start = 100 * zl + 25 * ylc_index()
    for n in range(25):
        flat = flat_start + n
        lens_row = (flat * 205) >> 14
        lens_col = flat - 80 * lens_row
        kind = (lens_col * 205) >> 12
        index = lens_col - 20 * kind
        regular = index < 16
        source = jnp.where(regular, index >> 1, 2 * kind + ((index - 16) >> 1))
        first = lens_row == zl + (kind < zl).astype(I32)
        unit = jnp.where(regular, jnp.where(first, 2 * kind, 10), jnp.where(first, 8, 12))
        place = 4 * (unit + (index & 1))
        block = got_ref[source]
        block = jnp.concatenate([block, block], axis=0)
        turned = [pltpu.roll(block, (n + 128 - q - place) & 127, axis=1) for q in range(4)]
        for h in range(2):
            pair = jnp.where(row < 4, turned[2 * h], turned[2 * h + 1])
            phases[h] = jnp.where(cell == n, pair, phases[h])
    re, im = [], []
    for h in range(2):
        light = light_ref[h]
        re.append(light * jnp.cos(phases[h]))
        im.append(light * jnp.sin(phases[h]))
    power = re[0] * re[0] + im[0] * im[0] + re[1] * re[1] + im[1] * im[1]
    flux = jnp.sum(power, axis=0, keepdims=True)
    along_p = -4.0 * power
    pixel = row & 3
    for h in range(2):
        for d in range(1, 4):
            back_re = pltpu.roll(re[h], d, axis=0)
            back_im = pltpu.roll(im[h], d, axis=0)
            same = re[h] * back_re + im[h] * back_im
            cross = im[h] * back_re - re[h] * back_im
            sign = -8.0 if d % 2 == 0 else 8.0
            term = sign * same + (4.0 * LAG[d - 1]) * cross
            along_p = along_p + jnp.where(pixel >= d, term, 0.0)
    swap_re = [pltpu.roll(x, 4, axis=0) for x in re]
    swap_im = [pltpu.roll(x, 4, axis=0) for x in im]

    def term_of(to_re, to_im, from_re, from_im, d):
        same = to_re * from_re + to_im * from_im
        cross = to_im * from_re - to_re * from_im
        sign = -8.0 if d % 2 == 0 else 8.0
        return sign * same + (4.0 * LAG[d - 1]) * cross

    along_q = -4.0 * power
    upper = row >= 4
    for h in range(2):
        along_q = along_q + jnp.where(upper, term_of(re[h], im[h], swap_re[h], swap_im[h], 1), 0.0)
    along_q = along_q + term_of(re[1], im[1], re[0], im[0], 2)
    near = term_of(re[1], im[1], swap_re[0], swap_im[0], 1)
    far = term_of(re[1], im[1], swap_re[0], swap_im[0], 3)
    along_q = along_q + jnp.where(upper, far, near)
    scale = 0.125 / flux
    slope_p = jnp.sum(along_p, axis=0, keepdims=True) * scale
    slope_q = jnp.sum(along_q, axis=0, keepdims=True) * scale
    pair = jnp.where(row == 0, slope_p, slope_q)
    compact = [pair, pltpu.roll(pair, 64, axis=1)]
    for frame in range(2):
        slopes_ref[frame] = compact[frame]
    total = jnp.zeros((8, ACTUATORS), F32)
    for axis in range(2):
        left = jnp.where(row == 0, compact[0][axis : axis + 1], compact[1][axis : axis + 1])
        left = left[:, 0:25].astype(BF16)
        total = total + jnp.dot(left, recon_ref[axis], preferred_element_type=F32)
    for j in range(32):
        start = 384 * (j % 16)
        width = min(384, ACTUATORS - start)
        if width < 384:
            out_ref[j] = jnp.zeros((1, 384), F32)
        out_ref[j, :, 0:width] = total[j // 16 : j // 16 + 1, start : start + width]


def sum_kernel(got_ref, out_ref):
    total = jnp.sum(got_ref[...], axis=0)
    for i in range(out_ref.shape[0]):
        out_ref[i] = total


def clip_kernel(got_ref, code_ref, slopes_ref, slopes_out, out_ref):
    slopes_out[...] = slopes_ref[:, 0:2, 0:25]
    for j in range(16):
        start = 384 * j
        width = min(384, ACTUATORS - start)
        limit = code_ref[start : start + width].reshape(1, width).astype(F32) * 0.125
        first = jnp.clip(0.5 * got_ref[j][:, 0:width], -limit, limit)
        second = jnp.clip(first + 0.5 * got_ref[16 + j][:, 0:width], -limit, limit)
        out_ref[0:1, start : start + width] = first
        out_ref[1:2, start : start + width] = second


def call(body, outs, specs, *args, scratch=(), name=None):
    return pl.pallas_call(
        body,
        out_shape=outs,
        in_specs=specs,
        out_specs=jax.tree.map(lambda _: VMEM, outs),
        scratch_shapes=list(scratch),
        compiler_params=pltpu.CompilerParams(vmem_limit_bytes=16 * 1024 * 1024),
        name=name,
    )(*args)


def exchange(value, axes):
    return lax.all_to_all(value, axes, 0, 0, tiled=True)


def shards(screens, row_offset, col_offset, layer_bin, illumination, reconstructor, sat_code):
    shape = jax.ShapeDtypeStruct
    row_offset = jnp.transpose(row_offset, (0, 2, 1))
    cols = call(columns_kernel, shape((32, 8, 256), F32), [VMEM, VMEM, VMEM], col_offset, layer_bin, screens, name="columns")
    cols = exchange(cols, PLANE)
    pupil, light = call(
        rows_kernel,
        (shape((16, 8, 128), F32), shape((2, 8, 128), F32)),
        [VMEM, VMEM, VMEM, VMEM],
        row_offset,
        layer_bin,
        illumination,
        cols,
        scratch=[pltpu.VMEM((16, 128), F32)],
        name="rows",
    )
    pupil = exchange(pupil, RING)
    owned = call(spread_kernel, shape((8, 4, 128), F32), [VMEM], pupil, name="spread")
    owned = exchange(owned, EIGHT)
    owned, reconstructor = lax.optimization_barrier((owned, reconstructor))
    slopes, updates = call(
        slopes_kernel,
        (shape((2, 8, 128), F32), shape((32, 1, 384), F32)),
        [VMEM, VMEM, VMEM],
        owned,
        light,
        reconstructor,
        name="slopes",
    )
    updates = exchange(updates, PLANE)
    updates = call(sum_kernel, shape((16, 1, 384), F32), [VMEM], updates, name="sum_plane")
    updates = exchange(updates, RING)
    updates = call(sum_kernel, shape((32, 1, 384), F32), [VMEM], updates, name="sum_ring")
    updates = exchange(updates, PLANE)
    return call(
        clip_kernel,
        (shape((2, 2, 25), F32), shape((2, ACTUATORS), F32)),
        [VMEM, VMEM, VMEM],
        updates,
        sat_code,
        slopes,
        name="clip",
    )


def solution(mesh):
    fine = Mesh(mesh.devices.reshape(SIZES), NAMES)
    placed = (
        P(ALT, STRIP, None),
        P(),
        P(),
        P(),
        P(None, ALT + STRIP),
        P(None, ALT + STRIP, None),
        P(),
    )
    return jax.shard_map(
        shards,
        mesh=fine,
        in_specs=placed,
        out_specs=(P(None, None, ALT + STRIP), P()),
        check_vma=False,
    )
```

```python
import jax
import jax.numpy as jnp
from jax import lax
from jax.experimental import pallas as pl
from jax.experimental.pallas import tpu as pltpu
from jax.sharding import Mesh, PartitionSpec as P

ACTUATORS = 6000
F32 = jnp.float32
BF16 = jnp.bfloat16
I32 = jnp.int32

NAMES = ("xh", "xl", "yh", "zh", "zl", "yl", "co")
SIZES = (2, 2, 2, 4, 4, 2, 2)
ALT = ("xh", "xl", "yh")
STRIP = ("zh", "zl", "yl", "co")
PLANE = ("xh", "xl", "yh", "yl", "co")
EIGHT = ("xl", "yl", "co")
RING = ("zh", "zl")

ROOT = 2.0**0.5
LAG = (2.0 + 2.0 * ROOT, -2.0, 2.0 * ROOT - 2.0)

VMEM = pl.BlockSpec(memory_space=pltpu.VMEM)


def iota(shape, dim):
    return lax.broadcasted_iota(I32, shape, dim)


def alt_index():
    return lax.axis_index("xh") * 4 + lax.axis_index("xl") * 2 + lax.axis_index("yh")


def ylc_index():
    return lax.axis_index("yl") * 2 + lax.axis_index("co")


def block_index():
    return lax.axis_index("xl") * 4 + ylc_index()


def columns_kernel(col_ref, bin_ref, screen_ref, out_ref):
    alt = alt_index()
    lane = iota((1, 512), 1)
    block = lane >> 6
    part = (lane & 63) >> 2
    more = 20 * (block >> 1) + 16 + 2 * (block & 1)
    lenslet = jnp.where(part < 8, 20 * (part >> 1) + 2 * block, more) + (part & 1)
    column = (4 * lenslet + (lane & 3)).astype(F32)
    position = iota((384, 512), 0).astype(F32)
    results = []
    bins = bin_ref[...].reshape(1, 16)
    lefts = [col_ref[frame, pl.ds(2 * alt, 2), :] for frame in range(2)]
    for layer in range(2):
        chosen = jnp.where(iota((1, 16), 1) == 2 * alt + layer, bins, 0).astype(F32)
        shrink = 1.0 - jnp.sum(chosen, axis=1, keepdims=True) * 0.03125
        weights = jnp.maximum(0.0, 1.0 - jnp.abs(position - column * shrink)).astype(BF16)
        rows = screen_ref[layer].astype(F32)
        parts = []
        for frame in range(2):
            for star in range(2):
                turned = pltpu.roll(rows, (512 - lefts[frame][layer, star]) & 511, axis=1)
                parts.append(turned[:, :384])
        stacked = jnp.concatenate(parts, axis=0).astype(BF16)
        results.append(jnp.dot(stacked, weights, preferred_element_type=F32))
    lane = iota((8, 128), 1)
    for star in range(2):
        for block in range(8):
            start = (block // 2) * 128
            back = (block % 2) * 64

            def piece(layer, frame, to):
                top = frame * 16 + star * 8
                value = results[layer][top : top + 8, start : start + 128]
                shift = (to - back) % 128
                return value if shift == 0 else pltpu.roll(value, shift, axis=1)

            main = jnp.where(lane < 40, piece(0, 0, 0), jnp.where(lane < 80, piece(0, 1, 40), piece(1, 0, 80)))
            rest = jnp.where(lane[0:4] < 64, piece(1, 1, 0)[0:4], piece(1, 1, 64)[4:8])
            for yh in range(2):
                to = star * 16 + (block // 4) * 8 + yh * 4 + block % 4
                out_ref[to, 0] = main[0:4]
                out_ref[to, 1] = main[4:8]
                out_ref[to, 2] = rest


def rows_kernel(row_ref, bin_ref, light_ref, got_ref, out_ref, light_out, scratch):
    star = lax.axis_index("xh")
    block = block_index()
    ring = lax.axis_index("zh") * 4 + lax.axis_index("zl")
    main = jnp.concatenate([got_ref[:, half].reshape(128, 128) for half in range(2)], axis=0)
    rest = got_ref[:, 2].reshape(128, 128)
    rest = jnp.concatenate([pltpu.roll(rest, 64, axis=1), rest], axis=0)
    left_half = iota((256, 128), 1) < 64
    rights = []
    for value in (
        jnp.where(left_half, main, pltpu.roll(main, 24, axis=1)),
        jnp.where(left_half, pltpu.roll(main, 48, axis=1), rest),
    ):
        high = value.astype(BF16)
        rights.append(jnp.concatenate([high, (value - high.astype(F32)).astype(BF16)], axis=1))
    line = iota((32, 1), 0)
    quarter = 2 * ((line >> 2) & 1) + lax.axis_index("yh")
    base = (80 * quarter + 20 * (line >> 3) + (line & 3)).astype(F32)
    pupil_row = jnp.concatenate([base + 4.0 * rr for rr in range(5)], axis=0)
    spot = iota((1, 256), 1)
    screen_row = (ring * 32 + 8 * ((spot >> 2) & 3) + 4 * (spot >> 7) + (spot & 3)).astype(F32)
    tops = [jnp.where(star == 0, row_ref[frame, 0:1, :], row_ref[frame, 1:2, :]) for frame in range(2)]
    parts = [top >> 4 for top in tops] + [top & 15 for top in tops] + [bin_ref[...].reshape(1, 16)]
    line16 = iota((8, 16), 0)
    packed = jnp.zeros((8, 16), F32)
    for n, part in enumerate(parts):
        packed = jnp.where(line16 == n, part.astype(F32), packed)
    packed = packed.astype(BF16)
    sums = [None, None]
    for layer in range(2):
        pick = (iota((16, 256), 0) == 2 * ((iota((16, 256), 1) >> 4) & 7) + layer).astype(F32).astype(BF16)
        lanes = jnp.dot(packed, pick, preferred_element_type=F32)
        scaled = pupil_row * (1.0 - lanes[4:5] * 0.03125)
        for frame in range(2):
            offset = screen_row - (16.0 * lanes[frame : frame + 1] + lanes[2 + frame : 3 + frame])
            weights = jnp.maximum(0.0, 1.0 - jnp.abs(offset - scaled)).astype(BF16)
            term = jnp.dot(weights, rights[layer], preferred_element_type=F32)
            sums[frame] = term if layer == 0 else sums[frame] + term
    sums = [total[:, :128] + total[:, 128:] for total in sums]
    merged = jnp.where(iota((160, 128), 1) < 64, sums[0], sums[1])
    cell = iota((8, 128), 1) & 63
    kind = jnp.where(cell < 32, cell >> 3, block >> 1)
    for t in range(4):
        pieces = [merged[rr * 32 + t * 8 : rr * 32 + t * 8 + 8] for rr in range(5)]
        for zl in range(4):
            here, after = pieces[zl], pieces[zl + 1]
            first = jnp.where(kind < zl, after, here)
            second = jnp.where(cell < 48, pltpu.roll(after, 40 - 8 * zl, axis=1), pltpu.roll(after, 16, axis=1))
            out_ref[t * 4 + zl] = jnp.where(cell < 40, first, second)
    scratch[...] = jnp.ones((16, 128), F32)
    scratch[:, 0:25] = light_ref[...]
    wide = scratch[...]
    inside = iota((16, 128), 1)
    scratch[...] = jnp.where((inside >= 64) & (inside < 89), pltpu.roll(wide, 64, axis=1), wide)
    for q in range(4):
        top = (q % 2) * 4
        light_out[q // 2, top : top + 4, :] = scratch[pl.ds(q, 4, stride=4), :]


def spread_kernel(got_ref, out_ref):
    total = jnp.sum(got_ref[...], axis=0)
    for to in range(8):
        top = (to // 4) * 4
        out_ref[to] = total[top : top + 4]


def slopes_kernel(got_ref, light_ref, recon_ref, slopes_ref, out_ref):
    zl = lax.axis_index("zl")
    row = iota((8, 128), 0)
    lane = iota((8, 128), 1)
    cell = lane & 63
    phases = [jnp.zeros((8, 128), F32), jnp.zeros((8, 128), F32)]
    flat_start = 100 * zl + 25 * ylc_index()
    for n in range(25):
        flat = flat_start + n
        lens_row = (flat * 205) >> 14
        lens_col = flat - 80 * lens_row
        kind = (lens_col * 205) >> 12
        index = lens_col - 20 * kind
        regular = index < 16
        source = jnp.where(regular, index >> 1, 2 * kind + ((index - 16) >> 1))
        first = lens_row == zl + (kind < zl).astype(I32)
        unit = jnp.where(regular, jnp.where(first, 2 * kind, 10), jnp.where(first, 8, 12))
        place = 4 * (unit + (index & 1))
        block = got_ref[source]
        block = jnp.concatenate([block, block], axis=0)
        turned = [pltpu.roll(block, (n + 128 - q - place) & 127, axis=1) for q in range(4)]
        for h in range(2):
            pair = jnp.where(row < 4, turned[2 * h], turned[2 * h + 1])
            phases[h] = jnp.where(cell == n, pair, phases[h])
    re, im = [], []
    for h in range(2):
        light = light_ref[h]
        re.append(light * jnp.cos(phases[h]))
        im.append(light * jnp.sin(phases[h]))
    power = re[0] * re[0] + im[0] * im[0] + re[1] * re[1] + im[1] * im[1]
    flux = jnp.sum(power, axis=0, keepdims=True)
    along_p = -4.0 * power
    pixel = row & 3
    for h in range(2):
        for d in range(1, 4):
            back_re = pltpu.roll(re[h], d, axis=0)
            back_im = pltpu.roll(im[h], d, axis=0)
            same = re[h] * back_re + im[h] * back_im
            cross = im[h] * back_re - re[h] * back_im
            sign = -8.0 if d % 2 == 0 else 8.0
            term = sign * same + (4.0 * LAG[d - 1]) * cross
            along_p = along_p + jnp.where(pixel >= d, term, 0.0)
    swap_re = [pltpu.roll(x, 4, axis=0) for x in re]
    swap_im = [pltpu.roll(x, 4, axis=0) for x in im]

    def term_of(to_re, to_im, from_re, from_im, d):
        same = to_re * from_re + to_im * from_im
        cross = to_im * from_re - to_re * from_im
        sign = -8.0 if d % 2 == 0 else 8.0
        return sign * same + (4.0 * LAG[d - 1]) * cross

    along_q = -4.0 * power
    upper = row >= 4
    for h in range(2):
        along_q = along_q + jnp.where(upper, term_of(re[h], im[h], swap_re[h], swap_im[h], 1), 0.0)
    along_q = along_q + term_of(re[1], im[1], re[0], im[0], 2)
    near = term_of(re[1], im[1], swap_re[0], swap_im[0], 1)
    far = term_of(re[1], im[1], swap_re[0], swap_im[0], 3)
    along_q = along_q + jnp.where(upper, far, near)
    scale = 0.125 / flux
    slope_p = jnp.sum(along_p, axis=0, keepdims=True) * scale
    slope_q = jnp.sum(along_q, axis=0, keepdims=True) * scale
    pair = jnp.where(row == 0, slope_p, slope_q)
    compact = [pair, pltpu.roll(pair, 64, axis=1)]
    for frame in range(2):
        slopes_ref[frame] = compact[frame]
    total = jnp.zeros((8, ACTUATORS), F32)
    for axis in range(2):
        left = jnp.where(row == 0, compact[0][axis : axis + 1], compact[1][axis : axis + 1])
        left = left[:, 0:25].astype(BF16)
        total = total + jnp.dot(left, recon_ref[axis], preferred_element_type=F32)
    for j in range(32):
        start = 384 * (j % 16)
        width = min(384, ACTUATORS - start)
        if width < 384:
            out_ref[j] = jnp.zeros((1, 384), F32)
        out_ref[j, :, 0:width] = total[j // 16 : j // 16 + 1, start : start + width]


def sum_kernel(got_ref, out_ref):
    total = jnp.sum(got_ref[...], axis=0)
    for i in range(out_ref.shape[0]):
        out_ref[i] = total


def clip_kernel(got_ref, code_ref, slopes_ref, slopes_out, out_ref):
    slopes_out[...] = slopes_ref[:, 0:2, 0:25]
    for j in range(16):
        start = 384 * j
        width = min(384, ACTUATORS - start)
        limit = code_ref[start : start + width].reshape(1, width).astype(F32) * 0.125
        first = jnp.clip(0.5 * got_ref[j][:, 0:width], -limit, limit)
        second = jnp.clip(first + 0.5 * got_ref[16 + j][:, 0:width], -limit, limit)
        out_ref[0:1, start : start + width] = first
        out_ref[1:2, start : start + width] = second


def call(body, outs, specs, *args, scratch=(), name=None):
    return pl.pallas_call(
        body,
        out_shape=outs,
        in_specs=specs,
        out_specs=jax.tree.map(lambda _: VMEM, outs),
        scratch_shapes=list(scratch),
        compiler_params=pltpu.CompilerParams(vmem_limit_bytes=16 * 1024 * 1024),
        name=name,
    )(*args)


def exchange(value, axes):
    return lax.all_to_all(value, axes, 0, 0, tiled=True)


def shards(screens, row_offset, col_offset, layer_bin, illumination, reconstructor, sat_code):
    shape = jax.ShapeDtypeStruct
    row_offset = jnp.transpose(row_offset, (0, 2, 1))
    cols = call(columns_kernel, shape((32, 3, 4, 128), F32), [VMEM, VMEM, VMEM], col_offset, layer_bin, screens, name="columns")
    cols = exchange(cols, PLANE)
    pupil, light = call(
        rows_kernel,
        (shape((16, 8, 128), F32), shape((2, 8, 128), F32)),
        [VMEM, VMEM, VMEM, VMEM],
        row_offset,
        layer_bin,
        illumination,
        cols,
        scratch=[pltpu.VMEM((16, 128), F32)],
        name="rows",
    )
    pupil = exchange(pupil, RING)
    owned = call(spread_kernel, shape((8, 4, 128), F32), [VMEM], pupil, name="spread")
    owned = exchange(owned, EIGHT)
    owned, reconstructor = lax.optimization_barrier((owned, reconstructor))
    slopes, updates = call(
        slopes_kernel,
        (shape((2, 8, 128), F32), shape((32, 1, 384), F32)),
        [VMEM, VMEM, VMEM],
        owned,
        light,
        reconstructor,
        name="slopes",
    )
    updates = exchange(updates, PLANE)
    updates = call(sum_kernel, shape((16, 1, 384), F32), [VMEM], updates, name="sum_plane")
    updates = exchange(updates, RING)
    updates = call(sum_kernel, shape((32, 1, 384), F32), [VMEM], updates, name="sum_ring")
    updates = exchange(updates, PLANE)
    return call(
        clip_kernel,
        (shape((2, 2, 25), F32), shape((2, ACTUATORS), F32)),
        [VMEM, VMEM, VMEM],
        updates,
        sat_code,
        slopes,
        name="clip",
    )


def solution(mesh):
    fine = Mesh(mesh.devices.reshape(SIZES), NAMES)
    placed = (
        P(ALT, STRIP, None),
        P(),
        P(),
        P(),
        P(None, ALT + STRIP),
        P(None, ALT + STRIP, None),
        P(),
    )
    return jax.shard_map(
        shards,
        mesh=fine,
        in_specs=placed,
        out_specs=(P(None, None, ALT + STRIP), P()),
        check_vma=False,
    )
```

```python
import jax
import jax.numpy as jnp
from jax import lax
from jax.experimental import pallas as pl
from jax.experimental.pallas import tpu as pltpu
from jax.sharding import Mesh, PartitionSpec as P

ACTUATORS = 6000
F32 = jnp.float32
BF16 = jnp.bfloat16
I32 = jnp.int32

NAMES = ("xh", "xl", "yh", "zh", "zl", "yl", "co")
SIZES = (2, 2, 2, 4, 4, 2, 2)
ALT = ("xh", "xl", "yh")
STRIP = ("zh", "zl", "yl", "co")
PLANE = ("xh", "xl", "yh", "yl", "co")
EIGHT = ("xl", "yl", "co")
RING = ("zh", "zl")

ROOT = 2.0**0.5
LAG = (2.0 + 2.0 * ROOT, -2.0, 2.0 * ROOT - 2.0)

VMEM = pl.BlockSpec(memory_space=pltpu.VMEM)


def iota(shape, dim):
    return lax.broadcasted_iota(I32, shape, dim)


def alt_index():
    return lax.axis_index("xh") * 4 + lax.axis_index("xl") * 2 + lax.axis_index("yh")


def ylc_index():
    return lax.axis_index("yl") * 2 + lax.axis_index("co")


def block_index():
    return lax.axis_index("xl") * 4 + ylc_index()


def columns_kernel(col_ref, bin_ref, screen_ref, out_ref):
    alt = alt_index()
    lane = iota((1, 512), 1)
    block = lane >> 6
    part = (lane & 63) >> 2
    more = 20 * (block >> 1) + 16 + 2 * (block & 1)
    lenslet = jnp.where(part < 8, 20 * (part >> 1) + 2 * block, more) + (part & 1)
    column = (4 * lenslet + (lane & 3)).astype(F32)
    position = iota((384, 512), 0).astype(F32)
    results = []
    bins = bin_ref[...].reshape(1, 16)
    lefts = [col_ref[frame, pl.ds(2 * alt, 2), :] for frame in range(2)]
    for layer in range(2):
        chosen = jnp.where(iota((1, 16), 1) == 2 * alt + layer, bins, 0).astype(F32)
        shrink = 1.0 - jnp.sum(chosen, axis=1, keepdims=True) * 0.03125
        weights = jnp.maximum(0.0, 1.0 - jnp.abs(position - column * shrink)).astype(BF16)
        rows = screen_ref[layer].astype(F32)
        parts = []
        for frame in range(2):
            for star in range(2):
                turned = pltpu.roll(rows, (512 - lefts[frame][layer, star]) & 511, axis=1)
                parts.append(turned[:, :384])
        stacked = jnp.concatenate(parts, axis=0).astype(BF16)
        results.append(jnp.dot(stacked, weights, preferred_element_type=F32))
    lane = iota((8, 128), 1)
    for star in range(2):
        for block in range(8):
            start = (block // 2) * 128
            back = (block % 2) * 64

            def piece(layer, frame, to):
                top = frame * 16 + star * 8
                value = results[layer][top : top + 8, start : start + 128]
                shift = (to - back) % 128
                return value if shift == 0 else pltpu.roll(value, shift, axis=1)

            main = jnp.where(lane < 40, piece(0, 0, 0), jnp.where(lane < 80, piece(0, 1, 40), piece(1, 0, 80)))
            rest = jnp.where(lane[0:4] < 64, piece(1, 1, 0)[0:4], piece(1, 1, 64)[4:8])
            for yh in range(2):
                to = star * 16 + (block // 4) * 8 + yh * 4 + block % 4
                out_ref[to, 0] = main[0:4]
                out_ref[to, 1] = main[4:8]
                out_ref[to, 2] = rest


def rows_kernel(row_ref, bin_ref, light_ref, got_ref, out_ref, light_out, scratch):
    star = lax.axis_index("xh")
    block = block_index()
    ring = lax.axis_index("zh") * 4 + lax.axis_index("zl")
    main = jnp.concatenate([got_ref[:, half].reshape(128, 128) for half in range(2)], axis=0)
    rest = got_ref[:, 2].reshape(128, 128)
    rest = jnp.concatenate([pltpu.roll(rest, 64, axis=1), rest], axis=0)
    left_half = iota((256, 128), 1) < 64
    rights = []
    for value in (
        jnp.where(left_half, main, pltpu.roll(main, 24, axis=1)),
        jnp.where(left_half, pltpu.roll(main, 48, axis=1), rest),
    ):
        high = value.astype(BF16)
        rights.append(jnp.concatenate([high, (value - high.astype(F32)).astype(BF16)], axis=1))
    line = iota((32, 1), 0)
    quarter = 2 * ((line >> 2) & 1) + lax.axis_index("yh")
    base = (80 * quarter + 20 * (line >> 3) + (line & 3)).astype(F32)
    pupil_row = jnp.concatenate([base + 4.0 * rr for rr in range(5)], axis=0)
    spot = iota((1, 256), 1)
    screen_row = (ring * 32 + 8 * ((spot >> 2) & 3) + 4 * (spot >> 7) + (spot & 3)).astype(F32)
    tops = [jnp.where(star == 0, row_ref[frame, 0:1, :], row_ref[frame, 1:2, :]) for frame in range(2)]
    parts = [top >> 4 for top in tops] + [top & 15 for top in tops] + [bin_ref[...].reshape(1, 16)]
    line16 = iota((8, 16), 0)
    packed = jnp.zeros((8, 16), F32)
    for n, part in enumerate(parts):
        packed = jnp.where(line16 == n, part.astype(F32), packed)
    packed = packed.astype(BF16)
    sums = [None, None]
    for layer in range(2):
        pick = (iota((16, 256), 0) == 2 * ((iota((16, 256), 1) >> 4) & 7) + layer).astype(F32).astype(BF16)
        lanes = jnp.dot(packed, pick, preferred_element_type=F32)
        scaled = pupil_row * (1.0 - lanes[4:5] * 0.03125)
        for frame in range(2):
            offset = screen_row - (16.0 * lanes[frame : frame + 1] + lanes[2 + frame : 3 + frame])
            weights = jnp.maximum(0.0, 1.0 - jnp.abs(offset - scaled)).astype(BF16)
            term = jnp.dot(weights, rights[layer], preferred_element_type=F32)
            sums[frame] = term if layer == 0 else sums[frame] + term
    sums = [total[:, :128] + total[:, 128:] for total in sums]
    merged = jnp.where(iota((160, 128), 1) < 64, sums[0], sums[1])
    cell = iota((8, 128), 1) & 63
    kind = jnp.where(cell < 32, cell >> 3, block >> 1)
    for t in range(4):
        pieces = [merged[rr * 32 + t * 8 : rr * 32 + t * 8 + 8] for rr in range(5)]
        for zl in range(4):
            here, after = pieces[zl], pieces[zl + 1]
            first = jnp.where(kind < zl, after, here)
            second = jnp.where(cell < 48, pltpu.roll(after, 40 - 8 * zl, axis=1), pltpu.roll(after, 16, axis=1))
            out_ref[t * 4 + zl] = jnp.where(cell < 40, first, second)
    scratch[...] = jnp.ones((16, 128), F32)
    scratch[:, 0:25] = light_ref[...]
    wide = scratch[...]
    inside = iota((16, 128), 1)
    scratch[...] = jnp.where((inside >= 64) & (inside < 89), pltpu.roll(wide, 64, axis=1), wide)
    for q in range(4):
        top = (q % 2) * 4
        light_out[q // 2, top : top + 4, :] = scratch[pl.ds(q, 4, stride=4), :]


def spread_kernel(got_ref, out_ref):
    total = jnp.sum(got_ref[...], axis=0)
    for to in range(8):
        top = (to // 4) * 4
        out_ref[to] = total[top : top + 4]


def slopes_kernel(got_ref, light_ref, recon_ref, slopes_ref, out_ref, scratch):
    zl = lax.axis_index("zl")
    row = iota((8, 128), 0)
    lane = iota((8, 128), 1)
    for source in range(8):
        block = got_ref[source]
        for q in range(4):
            scratch[source, 4 * q : 4 * q + 4] = block if q == 0 else pltpu.roll(block, 128 - q, axis=1)
    cell16 = iota((16, 128), 1) & 63
    phase = jnp.zeros((16, 128), F32)
    flat_start = 100 * zl + 25 * ylc_index()
    for five in range(5):
        flat = flat_start + 5 * five
        lens_row = (flat * 205) >> 14
        lens_col = flat - 80 * lens_row
        kind = (lens_col * 205) >> 12
        start = lens_col - 20 * kind
        first = lens_row == zl + (kind < zl).astype(I32)
        regular_place = jnp.where(first, 8 * kind, 40)
        more_place = jnp.where(first, 32, 48)
        inner = start < 15
        for j in range(5):
            n = 5 * five + j
            index = start + j
            source = index >> 1
            place = regular_place + 4 * (index & 1)
            if j > 0:
                source = jnp.where(inner, source, 2 * kind + (j - 1) // 2)
                place = jnp.where(inner, place, more_place + 4 * ((j - 1) % 2))
            phase = jnp.where(cell16 == n, pltpu.roll(scratch[source], (n + 128 - place) & 127, axis=1), phase)
    phases = [phase[0:8], phase[8:16]]
    re, im = [], []
    for h in range(2):
        light = light_ref[h]
        re.append(light * jnp.cos(phases[h]))
        im.append(light * jnp.sin(phases[h]))
    power = re[0] * re[0] + im[0] * im[0] + re[1] * re[1] + im[1] * im[1]
    flux = jnp.sum(power, axis=0, keepdims=True)
    along_p = -4.0 * power
    pixel = row & 3
    for h in range(2):
        for d in range(1, 4):
            back_re = pltpu.roll(re[h], d, axis=0)
            back_im = pltpu.roll(im[h], d, axis=0)
            same = re[h] * back_re + im[h] * back_im
            cross = im[h] * back_re - re[h] * back_im
            sign = -8.0 if d % 2 == 0 else 8.0
            term = sign * same + (4.0 * LAG[d - 1]) * cross
            along_p = along_p + jnp.where(pixel >= d, term, 0.0)
    swap_re = [pltpu.roll(x, 4, axis=0) for x in re]
    swap_im = [pltpu.roll(x, 4, axis=0) for x in im]

    def term_of(to_re, to_im, from_re, from_im, d):
        same = to_re * from_re + to_im * from_im
        cross = to_im * from_re - to_re * from_im
        sign = -8.0 if d % 2 == 0 else 8.0
        return sign * same + (4.0 * LAG[d - 1]) * cross

    along_q = -4.0 * power
    upper = row >= 4
    for h in range(2):
        along_q = along_q + jnp.where(upper, term_of(re[h], im[h], swap_re[h], swap_im[h], 1), 0.0)
    along_q = along_q + term_of(re[1], im[1], re[0], im[0], 2)
    near = term_of(re[1], im[1], swap_re[0], swap_im[0], 1)
    far = term_of(re[1], im[1], swap_re[0], swap_im[0], 3)
    along_q = along_q + jnp.where(upper, far, near)
    scale = 0.125 / flux
    slope_p = jnp.sum(along_p, axis=0, keepdims=True) * scale
    slope_q = jnp.sum(along_q, axis=0, keepdims=True) * scale
    pair = jnp.where(row == 0, slope_p, slope_q)
    compact = [pair, pltpu.roll(pair, 64, axis=1)]
    for frame in range(2):
        slopes_ref[frame] = compact[frame]
    total = jnp.zeros((8, ACTUATORS), F32)
    for axis in range(2):
        left = jnp.where(row == 0, compact[0][axis : axis + 1], compact[1][axis : axis + 1])
        left = left[:, 0:25].astype(BF16)
        total = total + jnp.dot(left, recon_ref[axis], preferred_element_type=F32)
    for j in range(32):
        start = 384 * (j % 16)
        width = min(384, ACTUATORS - start)
        if width < 384:
            out_ref[j] = jnp.zeros((1, 384), F32)
        out_ref[j, :, 0:width] = total[j // 16 : j // 16 + 1, start : start + width]


def sum_kernel(got_ref, out_ref):
    total = jnp.sum(got_ref[...], axis=0)
    for i in range(out_ref.shape[0]):
        out_ref[i] = total


def clip_kernel(got_ref, code_ref, slopes_ref, slopes_out, out_ref):
    slopes_out[...] = slopes_ref[:, 0:2, 0:25]
    for j in range(16):
        start = 384 * j
        width = min(384, ACTUATORS - start)
        limit = code_ref[start : start + width].reshape(1, width).astype(F32) * 0.125
        first = jnp.clip(0.5 * got_ref[j][:, 0:width], -limit, limit)
        second = jnp.clip(first + 0.5 * got_ref[16 + j][:, 0:width], -limit, limit)
        out_ref[0:1, start : start + width] = first
        out_ref[1:2, start : start + width] = second


def call(body, outs, specs, *args, scratch=(), name=None):
    return pl.pallas_call(
        body,
        out_shape=outs,
        in_specs=specs,
        out_specs=jax.tree.map(lambda _: VMEM, outs),
        scratch_shapes=list(scratch),
        compiler_params=pltpu.CompilerParams(vmem_limit_bytes=16 * 1024 * 1024),
        name=name,
    )(*args)


def exchange(value, axes):
    return lax.all_to_all(value, axes, 0, 0, tiled=True)


def shards(screens, row_offset, col_offset, layer_bin, illumination, reconstructor, sat_code):
    shape = jax.ShapeDtypeStruct
    row_offset = jnp.transpose(row_offset, (0, 2, 1))
    cols = call(columns_kernel, shape((32, 3, 4, 128), F32), [VMEM, VMEM, VMEM], col_offset, layer_bin, screens, name="columns")
    cols = exchange(cols, PLANE)
    pupil, light = call(
        rows_kernel,
        (shape((16, 8, 128), F32), shape((2, 8, 128), F32)),
        [VMEM, VMEM, VMEM, VMEM],
        row_offset,
        layer_bin,
        illumination,
        cols,
        scratch=[pltpu.VMEM((16, 128), F32)],
        name="rows",
    )
    pupil = exchange(pupil, RING)
    owned = call(spread_kernel, shape((8, 4, 128), F32), [VMEM], pupil, name="spread")
    owned = exchange(owned, EIGHT)
    owned, reconstructor = lax.optimization_barrier((owned, reconstructor))
    slopes, updates = call(
        slopes_kernel,
        (shape((2, 8, 128), F32), shape((32, 1, 384), F32)),
        [VMEM, VMEM, VMEM],
        owned,
        light,
        reconstructor,
        scratch=[pltpu.VMEM((8, 16, 128), F32)],
        name="slopes",
    )
    updates = exchange(updates, PLANE)
    updates = call(sum_kernel, shape((16, 1, 384), F32), [VMEM], updates, name="sum_plane")
    updates = exchange(updates, RING)
    updates = call(sum_kernel, shape((32, 1, 384), F32), [VMEM], updates, name="sum_ring")
    updates = exchange(updates, PLANE)
    return call(
        clip_kernel,
        (shape((2, 2, 25), F32), shape((2, ACTUATORS), F32)),
        [VMEM, VMEM, VMEM],
        updates,
        sat_code,
        slopes,
        name="clip",
    )


def solution(mesh):
    fine = Mesh(mesh.devices.reshape(SIZES), NAMES)
    placed = (
        P(ALT, STRIP, None),
        P(),
        P(),
        P(),
        P(None, ALT + STRIP),
        P(None, ALT + STRIP, None),
        P(),
    )
    return jax.shard_map(
        shards,
        mesh=fine,
        in_specs=placed,
        out_specs=(P(None, None, ALT + STRIP), P()),
        check_vma=False,
    )
```

```python
import jax
import jax.numpy as jnp
from jax import lax
from jax.experimental import pallas as pl
from jax.experimental.pallas import tpu as pltpu
from jax.sharding import Mesh, PartitionSpec as P

ACTUATORS = 6000
F32 = jnp.float32
BF16 = jnp.bfloat16
I32 = jnp.int32

NAMES = ("xh", "xl", "yh", "zh", "zl", "yl", "co")
SIZES = (2, 2, 2, 4, 4, 2, 2)
ALT = ("xh", "xl", "yh")
STRIP = ("zh", "zl", "yl", "co")
PLANE = ("xh", "xl", "yh", "yl", "co")
EIGHT = ("xl", "yl", "co")
RING = ("zh", "zl")

ROOT = 2.0**0.5
LAG = (2.0 + 2.0 * ROOT, -2.0, 2.0 * ROOT - 2.0)

VMEM = pl.BlockSpec(memory_space=pltpu.VMEM)


def iota(shape, dim):
    return lax.broadcasted_iota(I32, shape, dim)


def alt_index():
    return lax.axis_index("xh") * 4 + lax.axis_index("xl") * 2 + lax.axis_index("yh")


def ylc_index():
    return lax.axis_index("yl") * 2 + lax.axis_index("co")


def block_index():
    return lax.axis_index("xl") * 4 + ylc_index()


def columns_kernel(col_ref, bin_ref, screen_ref, out_ref):
    alt = alt_index()
    lane = iota((1, 512), 1)
    block = lane >> 6
    part = (lane & 63) >> 2
    more = 20 * (block >> 1) + 16 + 2 * (block & 1)
    lenslet = jnp.where(part < 8, 20 * (part >> 1) + 2 * block, more) + (part & 1)
    column = (4 * lenslet + (lane & 3)).astype(F32)
    position = iota((384, 512), 0).astype(F32)
    results = []
    bins = bin_ref[...].reshape(1, 16)
    lefts = [col_ref[frame, pl.ds(2 * alt, 2), :] for frame in range(2)]
    for layer in range(2):
        chosen = jnp.where(iota((1, 16), 1) == 2 * alt + layer, bins, 0).astype(F32)
        shrink = 1.0 - jnp.sum(chosen, axis=1, keepdims=True) * 0.03125
        weights = jnp.maximum(0.0, 1.0 - jnp.abs(position - column * shrink)).astype(BF16)
        rows = screen_ref[layer].astype(F32)
        parts = []
        for frame in range(2):
            for star in range(2):
                turned = pltpu.roll(rows, (512 - lefts[frame][layer, star]) & 511, axis=1)
                parts.append(turned[:, :384])
        stacked = jnp.concatenate(parts, axis=0).astype(BF16)
        results.append(jnp.dot(stacked, weights, preferred_element_type=F32))
    lane = iota((8, 128), 1)
    for star in range(2):
        for block in range(8):
            start = (block // 2) * 128
            back = (block % 2) * 64

            def piece(layer, frame, to):
                top = frame * 16 + star * 8
                value = results[layer][top : top + 8, start : start + 128]
                shift = (to - back) % 128
                return value if shift == 0 else pltpu.roll(value, shift, axis=1)

            main = jnp.where(lane < 40, piece(0, 0, 0), jnp.where(lane < 80, piece(0, 1, 40), piece(1, 0, 80)))
            rest = jnp.where(lane[0:4] < 64, piece(1, 1, 0)[0:4], piece(1, 1, 64)[4:8])
            for yh in range(2):
                to = star * 16 + (block // 4) * 8 + yh * 4 + block % 4
                out_ref[to, 0] = main[0:4]
                out_ref[to, 1] = main[4:8]
                out_ref[to, 2] = rest


def rows_kernel(row_ref, bin_ref, light_ref, got_ref, out_ref, light_out, scratch):
    star = lax.axis_index("xh")
    block = block_index()
    ring = lax.axis_index("zh") * 4 + lax.axis_index("zl")
    main = jnp.concatenate([got_ref[:, half].reshape(128, 128) for half in range(2)], axis=0)
    rest = got_ref[:, 2].reshape(128, 128)
    rest = jnp.concatenate([pltpu.roll(rest, 64, axis=1), rest], axis=0)
    left_half = iota((256, 128), 1) < 64
    rights = []
    for value in (
        jnp.where(left_half, main, pltpu.roll(main, 24, axis=1)),
        jnp.where(left_half, pltpu.roll(main, 48, axis=1), rest),
    ):
        high = value.astype(BF16)
        rights.append(jnp.concatenate([high, (value - high.astype(F32)).astype(BF16)], axis=1))
    line = iota((32, 1), 0)
    quarter = 2 * ((line >> 2) & 1) + lax.axis_index("yh")
    base = (80 * quarter + 20 * (line >> 3) + (line & 3)).astype(F32)
    pupil_row = jnp.concatenate([base + 4.0 * rr for rr in range(5)], axis=0)
    spot = iota((1, 256), 1)
    screen_row = (ring * 32 + 8 * ((spot >> 2) & 3) + 4 * (spot >> 7) + (spot & 3)).astype(F32)
    tops = [jnp.where(star == 0, row_ref[frame, 0:1, :], row_ref[frame, 1:2, :]) for frame in range(2)]
    parts = [top >> 4 for top in tops] + [top & 15 for top in tops] + [bin_ref[...].reshape(1, 16)]
    line16 = iota((8, 16), 0)
    packed = jnp.zeros((8, 16), F32)
    for n, part in enumerate(parts):
        packed = jnp.where(line16 == n, part.astype(F32), packed)
    packed = packed.astype(BF16)
    sums = [None, None]
    for layer in range(2):
        pick = (iota((16, 256), 0) == 2 * ((iota((16, 256), 1) >> 4) & 7) + layer).astype(F32).astype(BF16)
        lanes = jnp.dot(packed, pick, preferred_element_type=F32)
        scaled = pupil_row * (1.0 - lanes[4:5] * 0.03125)
        for frame in range(2):
            offset = screen_row - (16.0 * lanes[frame : frame + 1] + lanes[2 + frame : 3 + frame])
            weights = jnp.maximum(0.0, 1.0 - jnp.abs(offset - scaled)).astype(BF16)
            term = jnp.dot(weights, rights[layer], preferred_element_type=F32)
            sums[frame] = term if layer == 0 else sums[frame] + term
    sums = [total[:, :128] + total[:, 128:] for total in sums]
    merged = jnp.where(iota((160, 128), 1) < 64, sums[0], sums[1])
    lane = iota((8, 128), 1)
    cell = lane & 63
    kind = jnp.where(cell < 32, cell >> 3, block >> 1)
    for t in range(4):
        pieces = [merged[rr * 32 + t * 8 : rr * 32 + t * 8 + 8] for rr in range(5)]
        for zl in range(4):
            here, after = pieces[zl], pieces[zl + 1]
            first = jnp.where(kind < zl, after, here)
            second = jnp.where(cell < 48, pltpu.roll(after, 40 - 8 * zl, axis=1), pltpu.roll(after, 16, axis=1))
            value = jnp.where(cell < 40, first, second)
            value = jnp.where(lane < 56, value, pltpu.roll(value, 120, axis=1))
            last = pltpu.roll(jnp.broadcast_to(value[7:8], (8, 128)), 16, axis=1, stride=16, stride_axis=0)
            value = jnp.where(lane < 112, value, last)
            for n in range(7):
                out_ref[t * 4 + zl, n] = value[n : n + 1]
    scratch[...] = jnp.ones((16, 128), F32)
    scratch[:, 0:25] = light_ref[...]
    wide = scratch[...]
    inside = iota((16, 128), 1)
    scratch[...] = jnp.where((inside >= 64) & (inside < 89), pltpu.roll(wide, 64, axis=1), wide)
    for q in range(4):
        top = (q % 2) * 4
        light_out[q // 2, top : top + 4, :] = scratch[pl.ds(q, 4, stride=4), :]


def spread_kernel(got_ref, out_ref, scratch):
    total = jnp.sum(got_ref[...], axis=0)
    scratch[...] = jnp.zeros((16, 128), F32)
    for n in range(7):
        scratch[n : n + 1] = total[n]
        scratch[14 - n : 15 - n] = total[n]
    total = scratch[0:8]
    row = iota((8, 128), 0)
    lane = iota((8, 128), 1)
    ends = pltpu.roll(scratch[8:16], 16, axis=1, stride=16, stride_axis=0)
    last = jnp.sum(jnp.where((lane >> 4) == row, ends, 0.0), axis=0, keepdims=True)
    total = jnp.where(row == 7, last, total)
    total = jnp.where(lane < 64, total, pltpu.roll(total, 8, axis=1))
    for to in range(8):
        top = (to // 4) * 4
        out_ref[to] = total[top : top + 4]


def slopes_kernel(got_ref, light_ref, recon_ref, slopes_ref, out_ref, scratch):
    zl = lax.axis_index("zl")
    row = iota((8, 128), 0)
    lane = iota((8, 128), 1)
    for source in range(8):
        block = got_ref[source]
        for q in range(4):
            scratch[source, 4 * q : 4 * q + 4] = block if q == 0 else pltpu.roll(block, 128 - q, axis=1)
    cell16 = iota((16, 128), 1) & 63
    phase = jnp.zeros((16, 128), F32)
    flat_start = 100 * zl + 25 * ylc_index()
    for five in range(5):
        flat = flat_start + 5 * five
        lens_row = (flat * 205) >> 14
        lens_col = flat - 80 * lens_row
        kind = (lens_col * 205) >> 12
        start = lens_col - 20 * kind
        first = lens_row == zl + (kind < zl).astype(I32)
        regular_place = jnp.where(first, 8 * kind, 40)
        more_place = jnp.where(first, 32, 48)
        inner = start < 15
        for j in range(5):
            n = 5 * five + j
            index = start + j
            source = index >> 1
            place = regular_place + 4 * (index & 1)
            if j > 0:
                source = jnp.where(inner, source, 2 * kind + (j - 1) // 2)
                place = jnp.where(inner, place, more_place + 4 * ((j - 1) % 2))
            phase = jnp.where(cell16 == n, pltpu.roll(scratch[source], (n + 128 - place) & 127, axis=1), phase)
    phases = [phase[0:8], phase[8:16]]
    re, im = [], []
    for h in range(2):
        light = light_ref[h]
        re.append(light * jnp.cos(phases[h]))
        im.append(light * jnp.sin(phases[h]))
    power = re[0] * re[0] + im[0] * im[0] + re[1] * re[1] + im[1] * im[1]
    flux = jnp.sum(power, axis=0, keepdims=True)
    along_p = -4.0 * power
    pixel = row & 3
    for h in range(2):
        for d in range(1, 4):
            back_re = pltpu.roll(re[h], d, axis=0)
            back_im = pltpu.roll(im[h], d, axis=0)
            same = re[h] * back_re + im[h] * back_im
            cross = im[h] * back_re - re[h] * back_im
            sign = -8.0 if d % 2 == 0 else 8.0
            term = sign * same + (4.0 * LAG[d - 1]) * cross
            along_p = along_p + jnp.where(pixel >= d, term, 0.0)
    swap_re = [pltpu.roll(x, 4, axis=0) for x in re]
    swap_im = [pltpu.roll(x, 4, axis=0) for x in im]

    def term_of(to_re, to_im, from_re, from_im, d):
        same = to_re * from_re + to_im * from_im
        cross = to_im * from_re - to_re * from_im
        sign = -8.0 if d % 2 == 0 else 8.0
        return sign * same + (4.0 * LAG[d - 1]) * cross

    along_q = -4.0 * power
    upper = row >= 4
    for h in range(2):
        along_q = along_q + jnp.where(upper, term_of(re[h], im[h], swap_re[h], swap_im[h], 1), 0.0)
    along_q = along_q + term_of(re[1], im[1], re[0], im[0], 2)
    near = term_of(re[1], im[1], swap_re[0], swap_im[0], 1)
    far = term_of(re[1], im[1], swap_re[0], swap_im[0], 3)
    along_q = along_q + jnp.where(upper, far, near)
    scale = 0.125 / flux
    slope_p = jnp.sum(along_p, axis=0, keepdims=True) * scale
    slope_q = jnp.sum(along_q, axis=0, keepdims=True) * scale
    pair = jnp.where(row == 0, slope_p, slope_q)
    compact = [pair, pltpu.roll(pair, 64, axis=1)]
    for frame in range(2):
        slopes_ref[frame] = compact[frame]
    total = jnp.zeros((8, ACTUATORS), F32)
    for axis in range(2):
        left = jnp.where(row == 0, compact[0][axis : axis + 1], compact[1][axis : axis + 1])
        left = left[:, 0:25].astype(BF16)
        total = total + jnp.dot(left, recon_ref[axis], preferred_element_type=F32)
    for j in range(32):
        start = 384 * (j % 16)
        width = min(384, ACTUATORS - start)
        if width < 384:
            out_ref[j] = jnp.zeros((1, 384), F32)
        out_ref[j, :, 0:width] = total[j // 16 : j // 16 + 1, start : start + width]


def sum_kernel(got_ref, out_ref):
    total = jnp.sum(got_ref[...], axis=0)
    for i in range(out_ref.shape[0]):
        out_ref[i] = total


def clip_kernel(got_ref, code_ref, slopes_ref, slopes_out, out_ref):
    slopes_out[...] = slopes_ref[:, 0:2, 0:25]
    for j in range(16):
        start = 384 * j
        width = min(384, ACTUATORS - start)
        limit = code_ref[start : start + width].reshape(1, width).astype(F32) * 0.125
        first = jnp.clip(0.5 * got_ref[j][:, 0:width], -limit, limit)
        second = jnp.clip(first + 0.5 * got_ref[16 + j][:, 0:width], -limit, limit)
        out_ref[0:1, start : start + width] = first
        out_ref[1:2, start : start + width] = second


def call(body, outs, specs, *args, scratch=(), name=None):
    return pl.pallas_call(
        body,
        out_shape=outs,
        in_specs=specs,
        out_specs=jax.tree.map(lambda _: VMEM, outs),
        scratch_shapes=list(scratch),
        compiler_params=pltpu.CompilerParams(vmem_limit_bytes=16 * 1024 * 1024),
        name=name,
    )(*args)


def exchange(value, axes):
    return lax.all_to_all(value, axes, 0, 0, tiled=True)


def shards(screens, row_offset, col_offset, layer_bin, illumination, reconstructor, sat_code):
    shape = jax.ShapeDtypeStruct
    row_offset = jnp.transpose(row_offset, (0, 2, 1))
    cols = call(columns_kernel, shape((32, 3, 4, 128), F32), [VMEM, VMEM, VMEM], col_offset, layer_bin, screens, name="columns")
    cols = exchange(cols, PLANE)
    pupil, light = call(
        rows_kernel,
        (shape((16, 7, 1, 128), F32), shape((2, 8, 128), F32)),
        [VMEM, VMEM, VMEM, VMEM],
        row_offset,
        layer_bin,
        illumination,
        cols,
        scratch=[pltpu.VMEM((16, 128), F32)],
        name="rows",
    )
    pupil = exchange(pupil, RING)
    owned = call(spread_kernel, shape((8, 4, 128), F32), [VMEM], pupil, scratch=[pltpu.VMEM((16, 128), F32)], name="spread")
    owned = exchange(owned, EIGHT)
    owned, reconstructor = lax.optimization_barrier((owned, reconstructor))
    slopes, updates = call(
        slopes_kernel,
        (shape((2, 8, 128), F32), shape((32, 1, 384), F32)),
        [VMEM, VMEM, VMEM],
        owned,
        light,
        reconstructor,
        scratch=[pltpu.VMEM((8, 16, 128), F32)],
        name="slopes",
    )
    updates = exchange(updates, PLANE)
    updates = call(sum_kernel, shape((16, 1, 384), F32), [VMEM], updates, name="sum_plane")
    updates = exchange(updates, RING)
    updates = call(sum_kernel, shape((32, 1, 384), F32), [VMEM], updates, name="sum_ring")
    updates = exchange(updates, PLANE)
    return call(
        clip_kernel,
        (shape((2, 2, 25), F32), shape((2, ACTUATORS), F32)),
        [VMEM, VMEM, VMEM],
        updates,
        sat_code,
        slopes,
        name="clip",
    )


def solution(mesh):
    fine = Mesh(mesh.devices.reshape(SIZES), NAMES)
    placed = (
        P(ALT, STRIP, None),
        P(),
        P(),
        P(),
        P(None, ALT + STRIP),
        P(None, ALT + STRIP, None),
        P(),
    )
    return jax.shard_map(
        shards,
        mesh=fine,
        in_specs=placed,
        out_specs=(P(None, None, ALT + STRIP), P()),
        check_vma=False,
    )
```

```python
import jax
import jax.numpy as jnp
from jax import lax
from jax.experimental import pallas as pl
from jax.experimental.pallas import tpu as pltpu
from jax.sharding import Mesh, PartitionSpec as P

ACTUATORS = 6000
F32 = jnp.float32
BF16 = jnp.bfloat16
I32 = jnp.int32

NAMES = ("xh", "xl", "yh", "zh", "zl", "yl", "co")
SIZES = (2, 2, 2, 4, 4, 2, 2)
ALT = ("xh", "xl", "yh")
STRIP = ("zh", "zl", "yl", "co")
PLANE = ("xh", "xl", "yh", "yl", "co")
EIGHT = ("xl", "yl", "co")
RING = ("zh", "zl")

ROOT = 2.0**0.5
LAG = (2.0 + 2.0 * ROOT, -2.0, 2.0 * ROOT - 2.0)

VMEM = pl.BlockSpec(memory_space=pltpu.VMEM)


def iota(shape, dim):
    return lax.broadcasted_iota(I32, shape, dim)


def tent(offset):
    return jnp.maximum(BF16(0.0), BF16(1.0) - jnp.abs(offset.astype(BF16)))


def alt_index():
    return lax.axis_index("xh") * 4 + lax.axis_index("xl") * 2 + lax.axis_index("yh")


def ylc_index():
    return lax.axis_index("yl") * 2 + lax.axis_index("co")


def block_index():
    return lax.axis_index("xl") * 4 + ylc_index()


def columns_kernel(col_ref, bin_ref, screen_ref, out_ref):
    alt = alt_index()
    lane = iota((1, 512), 1)
    block = lane >> 6
    part = (lane & 63) >> 2
    more = 20 * (block >> 1) + 16 + 2 * (block & 1)
    lenslet = jnp.where(part < 8, 20 * (part >> 1) + 2 * block, more) + (part & 1)
    column = (4 * lenslet + (lane & 3)).astype(F32)
    position = iota((384, 512), 0).astype(F32)
    results = []
    bins = bin_ref[...].reshape(1, 16)
    lefts = [col_ref[frame, pl.ds(2 * alt, 2), :] for frame in range(2)]
    for layer in range(2):
        chosen = jnp.where(iota((1, 16), 1) == 2 * alt + layer, bins, 0).astype(F32)
        shrink = 1.0 - jnp.sum(chosen, axis=1, keepdims=True) * 0.03125
        weights = tent(position - column * shrink)
        rows = screen_ref[layer].astype(F32)
        parts = []
        for frame in range(2):
            for star in range(2):
                turned = pltpu.roll(rows, (512 - lefts[frame][layer, star]) & 511, axis=1)
                parts.append(turned[:, :384])
        stacked = jnp.concatenate(parts, axis=0).astype(BF16)
        results.append(jnp.dot(stacked, weights, preferred_element_type=F32))
    lane = iota((8, 128), 1)
    for star in range(2):
        for block in range(8):
            start = (block // 2) * 128
            back = (block % 2) * 64

            def piece(layer, frame, to):
                top = frame * 16 + star * 8
                value = results[layer][top : top + 8, start : start + 128]
                shift = (to - back) % 128
                return value if shift == 0 else pltpu.roll(value, shift, axis=1)

            main = jnp.where(lane < 40, piece(0, 0, 0), jnp.where(lane < 80, piece(0, 1, 40), piece(1, 0, 80)))
            rest = jnp.where(lane[0:4] < 64, piece(1, 1, 0)[0:4], piece(1, 1, 64)[4:8])
            for yh in range(2):
                to = star * 16 + (block // 4) * 8 + yh * 4 + block % 4
                out_ref[to, 0] = main[0:4]
                out_ref[to, 1] = main[4:8]
                out_ref[to, 2] = rest


def rows_kernel(row_ref, bin_ref, light_ref, got_ref, out_ref, light_out, scratch):
    star = lax.axis_index("xh")
    block = block_index()
    ring = lax.axis_index("zh") * 4 + lax.axis_index("zl")
    main = jnp.concatenate([got_ref[:, half].reshape(128, 128) for half in range(2)], axis=0)
    rest = got_ref[:, 2].reshape(128, 128)
    rest = jnp.concatenate([pltpu.roll(rest, 64, axis=1), rest], axis=0)
    left_half = iota((256, 128), 1) < 64
    rights = []
    for value in (
        jnp.where(left_half, main, pltpu.roll(main, 24, axis=1)),
        jnp.where(left_half, pltpu.roll(main, 48, axis=1), rest),
    ):
        high = value.astype(BF16)
        rights.append(jnp.concatenate([high, (value - high.astype(F32)).astype(BF16)], axis=1))
    line = iota((32, 1), 0)
    quarter = 2 * ((line >> 2) & 1) + lax.axis_index("yh")
    base = (80 * quarter + 20 * (line >> 3) + (line & 3)).astype(F32)
    pupil_row = jnp.concatenate([base + 4.0 * rr for rr in range(5)], axis=0)
    spot = iota((1, 256), 1)
    screen_row = (ring * 32 + 8 * ((spot >> 2) & 3) + 4 * (spot >> 7) + (spot & 3)).astype(F32)
    tops = [jnp.where(star == 0, row_ref[frame, 0:1, :], row_ref[frame, 1:2, :]) for frame in range(2)]
    parts = [top >> 4 for top in tops] + [top & 15 for top in tops] + [bin_ref[...].reshape(1, 16)]
    line16 = iota((8, 16), 0)
    packed = jnp.zeros((8, 16), F32)
    for n, part in enumerate(parts):
        packed = jnp.where(line16 == n, part.astype(F32), packed)
    packed = packed.astype(BF16)
    sums = [None, None]
    for layer in range(2):
        pick = (iota((16, 256), 0) == 2 * ((iota((16, 256), 1) >> 4) & 7) + layer).astype(F32).astype(BF16)
        lanes = jnp.dot(packed, pick, preferred_element_type=F32)
        scaled = pupil_row * (1.0 - lanes[4:5] * 0.03125)
        for frame in range(2):
            offset = screen_row - (16.0 * lanes[frame : frame + 1] + lanes[2 + frame : 3 + frame])
            weights = tent(offset - scaled)
            term = jnp.dot(weights, rights[layer], preferred_element_type=F32)
            sums[frame] = term if layer == 0 else sums[frame] + term
    sums = [total[:, :128] + total[:, 128:] for total in sums]
    merged = jnp.where(iota((160, 128), 1) < 64, sums[0], sums[1])
    lane = iota((8, 128), 1)
    cell = lane & 63
    kind = jnp.where(cell < 32, cell >> 3, block >> 1)
    for t in range(4):
        pieces = [merged[rr * 32 + t * 8 : rr * 32 + t * 8 + 8] for rr in range(5)]
        for zl in range(4):
            here, after = pieces[zl], pieces[zl + 1]
            first = jnp.where(kind < zl, after, here)
            second = jnp.where(cell < 48, pltpu.roll(after, 40 - 8 * zl, axis=1), pltpu.roll(after, 16, axis=1))
            value = jnp.where(cell < 40, first, second)
            value = jnp.where(lane < 56, value, pltpu.roll(value, 120, axis=1))
            last = pltpu.roll(jnp.broadcast_to(value[7:8], (8, 128)), 16, axis=1, stride=16, stride_axis=0)
            value = jnp.where(lane < 112, value, last)
            for n in range(7):
                out_ref[t * 4 + zl, n] = value[n : n + 1]
    scratch[...] = jnp.ones((16, 128), F32)
    scratch[:, 0:25] = light_ref[...]
    wide = scratch[...]
    inside = iota((16, 128), 1)
    scratch[...] = jnp.where((inside >= 64) & (inside < 89), pltpu.roll(wide, 64, axis=1), wide)
    for q in range(4):
        top = (q % 2) * 4
        light_out[q // 2, top : top + 4, :] = scratch[pl.ds(q, 4, stride=4), :]


def spread_kernel(got_ref, out_ref, scratch):
    total = jnp.sum(got_ref[...], axis=0)
    scratch[...] = jnp.zeros((16, 128), F32)
    for n in range(7):
        scratch[n : n + 1] = total[n]
        scratch[14 - n : 15 - n] = total[n]
    total = scratch[0:8]
    row = iota((8, 128), 0)
    lane = iota((8, 128), 1)
    ends = pltpu.roll(scratch[8:16], 16, axis=1, stride=16, stride_axis=0)
    last = jnp.sum(jnp.where((lane >> 4) == row, ends, 0.0), axis=0, keepdims=True)
    total = jnp.where(row == 7, last, total)
    total = jnp.where(lane < 64, total, pltpu.roll(total, 8, axis=1))
    for to in range(8):
        top = (to // 4) * 4
        out_ref[to] = total[top : top + 4]


def slopes_kernel(got_ref, light_ref, recon_ref, slopes_ref, out_ref, scratch):
    zl = lax.axis_index("zl")
    row = iota((8, 128), 0)
    lane = iota((8, 128), 1)
    for source in range(8):
        block = got_ref[source]
        for q in range(4):
            scratch[source, 4 * q : 4 * q + 4] = block if q == 0 else pltpu.roll(block, 128 - q, axis=1)
    cell16 = iota((16, 128), 1) & 63
    phase = jnp.zeros((16, 128), F32)
    flat_start = 100 * zl + 25 * ylc_index()
    for five in range(5):
        flat = flat_start + 5 * five
        lens_row = (flat * 205) >> 14
        lens_col = flat - 80 * lens_row
        kind = (lens_col * 205) >> 12
        start = lens_col - 20 * kind
        first = lens_row == zl + (kind < zl).astype(I32)
        regular_place = jnp.where(first, 8 * kind, 40)
        more_place = jnp.where(first, 32, 48)
        inner = start < 15
        for j in range(5):
            n = 5 * five + j
            index = start + j
            source = index >> 1
            place = regular_place + 4 * (index & 1)
            if j > 0:
                source = jnp.where(inner, source, 2 * kind + (j - 1) // 2)
                place = jnp.where(inner, place, more_place + 4 * ((j - 1) % 2))
            phase = jnp.where(cell16 == n, pltpu.roll(scratch[source], (n + 128 - place) & 127, axis=1), phase)
    phases = [phase[0:8], phase[8:16]]
    re, im = [], []
    for h in range(2):
        light = light_ref[h]
        re.append(light * jnp.cos(phases[h]))
        im.append(light * jnp.sin(phases[h]))
    power = re[0] * re[0] + im[0] * im[0] + re[1] * re[1] + im[1] * im[1]
    flux = jnp.sum(power, axis=0, keepdims=True)
    along_p = -4.0 * power
    pixel = row & 3
    for h in range(2):
        for d in range(1, 4):
            back_re = pltpu.roll(re[h], d, axis=0)
            back_im = pltpu.roll(im[h], d, axis=0)
            same = re[h] * back_re + im[h] * back_im
            cross = im[h] * back_re - re[h] * back_im
            sign = -8.0 if d % 2 == 0 else 8.0
            term = sign * same + (4.0 * LAG[d - 1]) * cross
            along_p = along_p + jnp.where(pixel >= d, term, 0.0)
    swap_re = [pltpu.roll(x, 4, axis=0) for x in re]
    swap_im = [pltpu.roll(x, 4, axis=0) for x in im]

    def term_of(to_re, to_im, from_re, from_im, d):
        same = to_re * from_re + to_im * from_im
        cross = to_im * from_re - to_re * from_im
        sign = -8.0 if d % 2 == 0 else 8.0
        return sign * same + (4.0 * LAG[d - 1]) * cross

    along_q = -4.0 * power
    upper = row >= 4
    for h in range(2):
        along_q = along_q + jnp.where(upper, term_of(re[h], im[h], swap_re[h], swap_im[h], 1), 0.0)
    along_q = along_q + term_of(re[1], im[1], re[0], im[0], 2)
    near = term_of(re[1], im[1], swap_re[0], swap_im[0], 1)
    far = term_of(re[1], im[1], swap_re[0], swap_im[0], 3)
    along_q = along_q + jnp.where(upper, far, near)
    scale = 0.125 / flux
    slope_p = jnp.sum(along_p, axis=0, keepdims=True) * scale
    slope_q = jnp.sum(along_q, axis=0, keepdims=True) * scale
    pair = jnp.where(row == 0, slope_p, slope_q)
    compact = [pair, pltpu.roll(pair, 64, axis=1)]
    for frame in range(2):
        slopes_ref[frame] = compact[frame]
    total = jnp.zeros((8, ACTUATORS), F32)
    for axis in range(2):
        left = jnp.where(row == 0, compact[0][axis : axis + 1], compact[1][axis : axis + 1])
        left = left[:, 0:25].astype(BF16)
        total = total + jnp.dot(left, recon_ref[axis], preferred_element_type=F32)
    for j in range(32):
        start = 384 * (j % 16)
        width = min(384, ACTUATORS - start)
        if width < 384:
            out_ref[j] = jnp.zeros((1, 384), F32)
        out_ref[j, :, 0:width] = total[j // 16 : j // 16 + 1, start : start + width]


def sum_kernel(got_ref, out_ref):
    total = jnp.sum(got_ref[...], axis=0)
    for i in range(out_ref.shape[0]):
        out_ref[i] = total


def clip_kernel(got_ref, code_ref, slopes_ref, slopes_out, out_ref):
    slopes_out[...] = slopes_ref[:, 0:2, 0:25]
    for j in range(16):
        start = 384 * j
        width = min(384, ACTUATORS - start)
        limit = code_ref[start : start + width].reshape(1, width).astype(F32) * 0.125
        first = jnp.clip(0.5 * got_ref[j][:, 0:width], -limit, limit)
        second = jnp.clip(first + 0.5 * got_ref[16 + j][:, 0:width], -limit, limit)
        out_ref[0:1, start : start + width] = first
        out_ref[1:2, start : start + width] = second


def call(body, outs, specs, *args, scratch=(), name=None):
    return pl.pallas_call(
        body,
        out_shape=outs,
        in_specs=specs,
        out_specs=jax.tree.map(lambda _: VMEM, outs),
        scratch_shapes=list(scratch),
        compiler_params=pltpu.CompilerParams(vmem_limit_bytes=16 * 1024 * 1024),
        name=name,
    )(*args)


def exchange(value, axes):
    return lax.all_to_all(value, axes, 0, 0, tiled=True)


def shards(screens, row_offset, col_offset, layer_bin, illumination, reconstructor, sat_code):
    shape = jax.ShapeDtypeStruct
    row_offset = jnp.transpose(row_offset, (0, 2, 1))
    cols = call(columns_kernel, shape((32, 3, 4, 128), F32), [VMEM, VMEM, VMEM], col_offset, layer_bin, screens, name="columns")
    cols = exchange(cols, PLANE)
    pupil, light = call(
        rows_kernel,
        (shape((16, 7, 1, 128), F32), shape((2, 8, 128), F32)),
        [VMEM, VMEM, VMEM, VMEM],
        row_offset,
        layer_bin,
        illumination,
        cols,
        scratch=[pltpu.VMEM((16, 128), F32)],
        name="rows",
    )
    pupil = exchange(pupil, RING)
    owned = call(spread_kernel, shape((8, 4, 128), F32), [VMEM], pupil, scratch=[pltpu.VMEM((16, 128), F32)], name="spread")
    owned = exchange(owned, EIGHT)
    owned, reconstructor = lax.optimization_barrier((owned, reconstructor))
    slopes, updates = call(
        slopes_kernel,
        (shape((2, 8, 128), F32), shape((32, 1, 384), F32)),
        [VMEM, VMEM, VMEM],
        owned,
        light,
        reconstructor,
        scratch=[pltpu.VMEM((8, 16, 128), F32)],
        name="slopes",
    )
    updates = exchange(updates, PLANE)
    updates = call(sum_kernel, shape((16, 1, 384), F32), [VMEM], updates, name="sum_plane")
    updates = exchange(updates, RING)
    updates = call(sum_kernel, shape((32, 1, 384), F32), [VMEM], updates, name="sum_ring")
    updates = exchange(updates, PLANE)
    return call(
        clip_kernel,
        (shape((2, 2, 25), F32), shape((2, ACTUATORS), F32)),
        [VMEM, VMEM, VMEM],
        updates,
        sat_code,
        slopes,
        name="clip",
    )


def solution(mesh):
    fine = Mesh(mesh.devices.reshape(SIZES), NAMES)
    placed = (
        P(ALT, STRIP, None),
        P(),
        P(),
        P(),
        P(None, ALT + STRIP),
        P(None, ALT + STRIP, None),
        P(),
    )
    return jax.shard_map(
        shards,
        mesh=fine,
        in_specs=placed,
        out_specs=(P(None, None, ALT + STRIP), P()),
        check_vma=False,
    )
```

```python
import jax
import jax.numpy as jnp
from jax import lax
from jax.experimental import pallas as pl
from jax.experimental.pallas import tpu as pltpu
from jax.sharding import Mesh, PartitionSpec as P

ACTUATORS = 6000
F32 = jnp.float32
BF16 = jnp.bfloat16
I32 = jnp.int32

NAMES = ("xh", "xl", "yh", "zh", "zl", "yl", "co")
SIZES = (2, 2, 2, 4, 4, 2, 2)
ALT = ("xh", "xl", "yh")
STRIP = ("zh", "zl", "yl", "co")
PLANE = ("xh", "xl", "yh", "yl", "co")
EIGHT = ("xl", "yl", "co")
RING = ("zh", "zl")

ROOT = 2.0**0.5
LAG = (2.0 + 2.0 * ROOT, -2.0, 2.0 * ROOT - 2.0)

VMEM = pl.BlockSpec(memory_space=pltpu.VMEM)


def iota(shape, dim):
    return lax.broadcasted_iota(I32, shape, dim)


def tent(offset):
    return jnp.maximum(BF16(0.0), BF16(1.0) - jnp.abs(offset.astype(BF16)))


def alt_index():
    return lax.axis_index("xh") * 4 + lax.axis_index("xl") * 2 + lax.axis_index("yh")


def ylc_index():
    return lax.axis_index("yl") * 2 + lax.axis_index("co")


def block_index():
    return lax.axis_index("xl") * 4 + ylc_index()


def columns_kernel(col_ref, bin_ref, screen_ref, out_ref):
    alt = alt_index()
    lane = iota((1, 512), 1)
    block = lane >> 6
    part = (lane & 63) >> 2
    more = 20 * (block >> 1) + 16 + 2 * (block & 1)
    lenslet = jnp.where(part < 8, 20 * (part >> 1) + 2 * block, more) + (part & 1)
    column = (4 * lenslet + (lane & 3)).astype(F32)
    position = iota((384, 512), 0).astype(F32)
    results = []
    bins = bin_ref[...].reshape(1, 16)
    lefts = [col_ref[frame, pl.ds(2 * alt, 2), :] for frame in range(2)]
    for layer in range(2):
        chosen = jnp.where(iota((1, 16), 1) == 2 * alt + layer, bins, 0).astype(F32)
        shrink = 1.0 - jnp.sum(chosen, axis=1, keepdims=True) * 0.03125
        weights = tent(position - column * shrink)
        rows = screen_ref[layer].astype(F32)
        parts = []
        for frame in range(2):
            for star in range(2):
                turned = pltpu.roll(rows, (512 - lefts[frame][layer, star]) & 511, axis=1)
                parts.append(turned[:, :384])
        stacked = jnp.concatenate(parts, axis=0).astype(BF16)
        results.append(jnp.dot(stacked, weights, preferred_element_type=F32))
    lane = iota((8, 128), 1)
    for star in range(2):
        for block in range(8):
            start = (block // 2) * 128
            back = (block % 2) * 64

            def piece(layer, frame, to):
                top = frame * 16 + star * 8
                value = results[layer][top : top + 8, start : start + 128]
                shift = (to - back) % 128
                return value if shift == 0 else pltpu.roll(value, shift, axis=1)

            main = jnp.where(lane < 40, piece(0, 0, 0), jnp.where(lane < 80, piece(0, 1, 40), piece(1, 0, 80)))
            rest = jnp.where(lane[0:4] < 64, piece(1, 1, 0)[0:4], piece(1, 1, 64)[4:8])
            for yh in range(2):
                to = star * 16 + (block // 4) * 8 + yh * 4 + block % 4
                out_ref[to, 0] = main[0:4]
                out_ref[to, 1] = main[4:8]
                out_ref[to, 2] = rest


def rows_kernel(row_ref, bin_ref, light_ref, got_ref, out_ref, light_out, scratch):
    star = lax.axis_index("xh")
    block = block_index()
    ring = lax.axis_index("zh") * 4 + lax.axis_index("zl")
    main = jnp.concatenate([got_ref[:, half].reshape(128, 128) for half in range(2)], axis=0)
    rest = got_ref[:, 2].reshape(128, 128)
    rest = jnp.concatenate([pltpu.roll(rest, 56, axis=1), pltpu.roll(rest, 120, axis=1)], axis=0)
    left_half = iota((256, 128), 1) < 56
    rights = []
    for value in (
        jnp.where(left_half, main, pltpu.roll(main, 16, axis=1)),
        jnp.where(left_half, pltpu.roll(main, 48, axis=1), rest),
    ):
        high = value.astype(BF16)
        rights.append(jnp.concatenate([high, (value - high.astype(F32)).astype(BF16)], axis=1))
    line = iota((32, 1), 0)
    quarter = 2 * ((line >> 2) & 1) + lax.axis_index("yh")
    base = (80 * quarter + 20 * (line >> 3) + (line & 3)).astype(F32)
    pupil_row = jnp.concatenate([base + 4.0 * rr for rr in range(5)], axis=0)
    spot = iota((1, 256), 1)
    screen_row = (ring * 32 + 8 * ((spot >> 2) & 3) + 4 * (spot >> 7) + (spot & 3)).astype(F32)
    tops = [jnp.where(star == 0, row_ref[frame, 0:1, :], row_ref[frame, 1:2, :]) for frame in range(2)]
    parts = [top >> 4 for top in tops] + [top & 15 for top in tops] + [bin_ref[...].reshape(1, 16)]
    line16 = iota((8, 16), 0)
    packed = jnp.zeros((8, 16), F32)
    for n, part in enumerate(parts):
        packed = jnp.where(line16 == n, part.astype(F32), packed)
    packed = packed.astype(BF16)
    sums = [None, None]
    for layer in range(2):
        pick = (iota((16, 256), 0) == 2 * ((iota((16, 256), 1) >> 4) & 7) + layer).astype(F32).astype(BF16)
        lanes = jnp.dot(packed, pick, preferred_element_type=F32)
        scaled = pupil_row * (1.0 - lanes[4:5] * 0.03125)
        for frame in range(2):
            offset = screen_row - (16.0 * lanes[frame : frame + 1] + lanes[2 + frame : 3 + frame])
            weights = tent(offset - scaled)
            term = jnp.dot(weights, rights[layer], preferred_element_type=F32)
            sums[frame] = term if layer == 0 else sums[frame] + term
    sums = [total[:, :128] + total[:, 128:] for total in sums]
    merged = jnp.where(iota((160, 128), 1) < 56, sums[0], sums[1])
    lane = iota((8, 128), 1)
    cell = jnp.where(lane < 56, lane, lane - 56)
    kind = jnp.where(cell < 32, cell >> 3, block >> 1)
    for t in range(4):
        pieces = [merged[rr * 32 + t * 8 : rr * 32 + t * 8 + 8] for rr in range(5)]
        for zl in range(4):
            here, after = pieces[zl], pieces[zl + 1]
            first = jnp.where(kind < zl, after, here)
            second = jnp.where(cell < 48, pltpu.roll(after, 40 - 8 * zl, axis=1), pltpu.roll(after, 16, axis=1))
            value = jnp.where(cell < 40, first, second)
            last = pltpu.roll(jnp.broadcast_to(value[7:8], (8, 128)), 16, axis=1, stride=16, stride_axis=0)
            value = jnp.where(lane < 112, value, last)
            for n in range(7):
                out_ref[t * 4 + zl, n] = value[n : n + 1]
    scratch[...] = jnp.ones((16, 128), F32)
    scratch[:, 0:25] = light_ref[...]
    wide = scratch[...]
    inside = iota((16, 128), 1)
    scratch[...] = jnp.where((inside >= 64) & (inside < 89), pltpu.roll(wide, 64, axis=1), wide)
    for q in range(4):
        top = (q % 2) * 4
        light_out[q // 2, top : top + 4, :] = scratch[pl.ds(q, 4, stride=4), :]


def spread_kernel(got_ref, out_ref, scratch):
    total = jnp.sum(got_ref[...], axis=0)
    scratch[...] = jnp.zeros((16, 128), F32)
    for n in range(7):
        scratch[n : n + 1] = total[n]
        scratch[14 - n : 15 - n] = total[n]
    total = scratch[0:8]
    row = iota((8, 128), 0)
    lane = iota((8, 128), 1)
    ends = pltpu.roll(scratch[8:16], 16, axis=1, stride=16, stride_axis=0)
    last = jnp.sum(jnp.where((lane >> 4) == row, ends, 0.0), axis=0, keepdims=True)
    total = jnp.where(row == 7, last, total)
    total = jnp.where(lane < 64, total, pltpu.roll(total, 8, axis=1))
    for to in range(8):
        top = (to // 4) * 4
        out_ref[to] = total[top : top + 4]


def slopes_kernel(got_ref, light_ref, recon_ref, slopes_ref, out_ref, scratch):
    zl = lax.axis_index("zl")
    row = iota((8, 128), 0)
    lane = iota((8, 128), 1)
    for source in range(8):
        block = got_ref[source]
        for q in range(4):
            scratch[source, 4 * q : 4 * q + 4] = block if q == 0 else pltpu.roll(block, 128 - q, axis=1)
    cell16 = iota((16, 128), 1) & 63
    phase = jnp.zeros((16, 128), F32)
    flat_start = 100 * zl + 25 * ylc_index()
    for five in range(5):
        flat = flat_start + 5 * five
        lens_row = (flat * 205) >> 14
        lens_col = flat - 80 * lens_row
        kind = (lens_col * 205) >> 12
        start = lens_col - 20 * kind
        first = lens_row == zl + (kind < zl).astype(I32)
        regular_place = jnp.where(first, 8 * kind, 40)
        more_place = jnp.where(first, 32, 48)
        inner = start < 15
        for j in range(5):
            n = 5 * five + j
            index = start + j
            source = index >> 1
            place = regular_place + 4 * (index & 1)
            if j > 0:
                source = jnp.where(inner, source, 2 * kind + (j - 1) // 2)
                place = jnp.where(inner, place, more_place + 4 * ((j - 1) % 2))
            phase = jnp.where(cell16 == n, pltpu.roll(scratch[source], (n + 128 - place) & 127, axis=1), phase)
    phases = [phase[0:8], phase[8:16]]
    re, im = [], []
    for h in range(2):
        light = light_ref[h]
        re.append(light * jnp.cos(phases[h]))
        im.append(light * jnp.sin(phases[h]))
    power = re[0] * re[0] + im[0] * im[0] + re[1] * re[1] + im[1] * im[1]
    flux = jnp.sum(power, axis=0, keepdims=True)
    along_p = -4.0 * power
    pixel = row & 3
    for h in range(2):
        for d in range(1, 4):
            back_re = pltpu.roll(re[h], d, axis=0)
            back_im = pltpu.roll(im[h], d, axis=0)
            same = re[h] * back_re + im[h] * back_im
            cross = im[h] * back_re - re[h] * back_im
            sign = -8.0 if d % 2 == 0 else 8.0
            term = sign * same + (4.0 * LAG[d - 1]) * cross
            along_p = along_p + jnp.where(pixel >= d, term, 0.0)
    swap_re = [pltpu.roll(x, 4, axis=0) for x in re]
    swap_im = [pltpu.roll(x, 4, axis=0) for x in im]

    def term_of(to_re, to_im, from_re, from_im, d):
        same = to_re * from_re + to_im * from_im
        cross = to_im * from_re - to_re * from_im
        sign = -8.0 if d % 2 == 0 else 8.0
        return sign * same + (4.0 * LAG[d - 1]) * cross

    along_q = -4.0 * power
    upper = row >= 4
    for h in range(2):
        along_q = along_q + jnp.where(upper, term_of(re[h], im[h], swap_re[h], swap_im[h], 1), 0.0)
    along_q = along_q + term_of(re[1], im[1], re[0], im[0], 2)
    near = term_of(re[1], im[1], swap_re[0], swap_im[0], 1)
    far = term_of(re[1], im[1], swap_re[0], swap_im[0], 3)
    along_q = along_q + jnp.where(upper, far, near)
    scale = 0.125 / flux
    slope_p = jnp.sum(along_p, axis=0, keepdims=True) * scale
    slope_q = jnp.sum(along_q, axis=0, keepdims=True) * scale
    pair = jnp.where(row == 0, slope_p, slope_q)
    compact = [pair, pltpu.roll(pair, 64, axis=1)]
    for frame in range(2):
        slopes_ref[frame] = compact[frame]
    total = jnp.zeros((8, ACTUATORS), F32)
    for axis in range(2):
        left = jnp.where(row == 0, compact[0][axis : axis + 1], compact[1][axis : axis + 1])
        left = left[:, 0:25].astype(BF16)
        total = total + jnp.dot(left, recon_ref[axis], preferred_element_type=F32)
    for j in range(32):
        start = 384 * (j % 16)
        width = min(384, ACTUATORS - start)
        if width < 384:
            out_ref[j] = jnp.zeros((1, 384), F32)
        out_ref[j, :, 0:width] = total[j // 16 : j // 16 + 1, start : start + width]


def sum_kernel(got_ref, out_ref):
    total = jnp.sum(got_ref[...], axis=0)
    for i in range(out_ref.shape[0]):
        out_ref[i] = total


def clip_kernel(got_ref, code_ref, slopes_ref, slopes_out, out_ref):
    slopes_out[...] = slopes_ref[:, 0:2, 0:25]
    for j in range(16):
        start = 384 * j
        width = min(384, ACTUATORS - start)
        limit = code_ref[start : start + width].reshape(1, width).astype(F32) * 0.125
        first = jnp.clip(0.5 * got_ref[j][:, 0:width], -limit, limit)
        second = jnp.clip(first + 0.5 * got_ref[16 + j][:, 0:width], -limit, limit)
        out_ref[0:1, start : start + width] = first
        out_ref[1:2, start : start + width] = second


def call(body, outs, specs, *args, scratch=(), name=None):
    return pl.pallas_call(
        body,
        out_shape=outs,
        in_specs=specs,
        out_specs=jax.tree.map(lambda _: VMEM, outs),
        scratch_shapes=list(scratch),
        compiler_params=pltpu.CompilerParams(vmem_limit_bytes=16 * 1024 * 1024),
        name=name,
    )(*args)


def exchange(value, axes):
    return lax.all_to_all(value, axes, 0, 0, tiled=True)


def shards(screens, row_offset, col_offset, layer_bin, illumination, reconstructor, sat_code):
    shape = jax.ShapeDtypeStruct
    row_offset = jnp.transpose(row_offset, (0, 2, 1))
    cols = call(columns_kernel, shape((32, 3, 4, 128), F32), [VMEM, VMEM, VMEM], col_offset, layer_bin, screens, name="columns")
    cols = exchange(cols, PLANE)
    pupil, light = call(
        rows_kernel,
        (shape((16, 7, 1, 128), F32), shape((2, 8, 128), F32)),
        [VMEM, VMEM, VMEM, VMEM],
        row_offset,
        layer_bin,
        illumination,
        cols,
        scratch=[pltpu.VMEM((16, 128), F32)],
        name="rows",
    )
    pupil = exchange(pupil, RING)
    owned = call(spread_kernel, shape((8, 4, 128), F32), [VMEM], pupil, scratch=[pltpu.VMEM((16, 128), F32)], name="spread")
    owned = exchange(owned, EIGHT)
    owned, reconstructor = lax.optimization_barrier((owned, reconstructor))
    slopes, updates = call(
        slopes_kernel,
        (shape((2, 8, 128), F32), shape((32, 1, 384), F32)),
        [VMEM, VMEM, VMEM],
        owned,
        light,
        reconstructor,
        scratch=[pltpu.VMEM((8, 16, 128), F32)],
        name="slopes",
    )
    updates = exchange(updates, PLANE)
    updates = call(sum_kernel, shape((16, 1, 384), F32), [VMEM], updates, name="sum_plane")
    updates = exchange(updates, RING)
    updates = call(sum_kernel, shape((32, 1, 384), F32), [VMEM], updates, name="sum_ring")
    updates = exchange(updates, PLANE)
    return call(
        clip_kernel,
        (shape((2, 2, 25), F32), shape((2, ACTUATORS), F32)),
        [VMEM, VMEM, VMEM],
        updates,
        sat_code,
        slopes,
        name="clip",
    )


def solution(mesh):
    fine = Mesh(mesh.devices.reshape(SIZES), NAMES)
    placed = (
        P(ALT, STRIP, None),
        P(),
        P(),
        P(),
        P(None, ALT + STRIP),
        P(None, ALT + STRIP, None),
        P(),
    )
    return jax.shard_map(
        shards,
        mesh=fine,
        in_specs=placed,
        out_specs=(P(None, None, ALT + STRIP), P()),
        check_vma=False,
    )
```

```python
import jax
import jax.numpy as jnp
from jax import lax
from jax.experimental import pallas as pl
from jax.experimental.pallas import tpu as pltpu
from jax.sharding import Mesh, PartitionSpec as P

ACTUATORS = 6000
F32 = jnp.float32
BF16 = jnp.bfloat16
I32 = jnp.int32

NAMES = ("xh", "xl", "yh", "zh", "zl", "yl", "co")
SIZES = (2, 2, 2, 4, 4, 2, 2)
ALT = ("xh", "xl", "yh")
STRIP = ("zh", "zl", "yl", "co")
PLANE = ("xh", "xl", "yh", "yl", "co")
EIGHT = ("xl", "yl", "co")
RING = ("zh", "zl")

ROOT = 2.0**0.5
LAG = (2.0 + 2.0 * ROOT, -2.0, 2.0 * ROOT - 2.0)

VMEM = pl.BlockSpec(memory_space=pltpu.VMEM)


def iota(shape, dim):
    return lax.broadcasted_iota(I32, shape, dim)


def tent(offset):
    return jnp.maximum(BF16(0.0), BF16(1.0) - jnp.abs(offset.astype(BF16)))


def alt_index():
    return lax.axis_index("xh") * 4 + lax.axis_index("xl") * 2 + lax.axis_index("yh")


def ylc_index():
    return lax.axis_index("yl") * 2 + lax.axis_index("co")


def block_index():
    return lax.axis_index("xl") * 4 + ylc_index()


def columns_kernel(col_ref, bin_ref, screen_ref, out_ref):
    alt = alt_index()
    lane = iota((1, 512), 1)
    block = lane >> 6
    part = (lane & 63) >> 2
    more = 20 * (block >> 1) + 16 + 2 * (block & 1)
    lenslet = jnp.where(part < 8, 20 * (part >> 1) + 2 * block, more) + (part & 1)
    column = (4 * lenslet + (lane & 3)).astype(F32)
    position = iota((336, 512), 0).astype(F32)
    results = []
    bins = bin_ref[...].reshape(1, 16)
    lefts = [col_ref[frame, pl.ds(2 * alt, 2), :] for frame in range(2)]
    for layer in range(2):
        chosen = jnp.where(iota((1, 16), 1) == 2 * alt + layer, bins, 0).astype(F32)
        shrink = 1.0 - jnp.sum(chosen, axis=1, keepdims=True) * 0.03125
        weights = tent(position - column * shrink)
        rows = screen_ref[layer].astype(F32)
        parts = []
        for frame in range(2):
            for star in range(2):
                turned = pltpu.roll(rows, (512 - lefts[frame][layer, star]) & 511, axis=1)
                parts.append(turned[:, :336])
        stacked = jnp.concatenate(parts, axis=0).astype(BF16)
        results.append(jnp.dot(stacked, weights, preferred_element_type=F32))
    lane = iota((8, 128), 1)
    for star in range(2):
        for block in range(8):
            start = (block // 2) * 128
            back = (block % 2) * 64

            def piece(layer, frame, to):
                top = frame * 16 + star * 8
                value = results[layer][top : top + 8, start : start + 128]
                shift = (to - back) % 128
                return value if shift == 0 else pltpu.roll(value, shift, axis=1)

            main = jnp.where(lane < 40, piece(0, 0, 0), jnp.where(lane < 80, piece(0, 1, 40), piece(1, 0, 80)))
            rest = jnp.where(lane[0:4] < 64, piece(1, 1, 0)[0:4], piece(1, 1, 64)[4:8])
            for yh in range(2):
                to = star * 16 + (block // 4) * 8 + yh * 4 + block % 4
                out_ref[to, 0] = main[0:4]
                out_ref[to, 1] = main[4:8]
                out_ref[to, 2] = rest


def rows_kernel(row_ref, bin_ref, light_ref, got_ref, out_ref, light_out, scratch):
    star = lax.axis_index("xh")
    block = block_index()
    ring = lax.axis_index("zh") * 4 + lax.axis_index("zl")
    main = jnp.concatenate([got_ref[:, half].reshape(128, 128) for half in range(2)], axis=0)
    rest = got_ref[:, 2].reshape(128, 128)
    rest = jnp.concatenate([pltpu.roll(rest, 56, axis=1), pltpu.roll(rest, 120, axis=1)], axis=0)
    left_half = iota((256, 128), 1) < 56
    rights = []
    for value in (
        jnp.where(left_half, main, pltpu.roll(main, 16, axis=1)),
        jnp.where(left_half, pltpu.roll(main, 48, axis=1), rest),
    ):
        high = value.astype(BF16)
        rights.append(jnp.concatenate([high, (value - high.astype(F32)).astype(BF16)], axis=1))
    line = iota((32, 1), 0)
    quarter = 2 * ((line >> 2) & 1) + lax.axis_index("yh")
    base = (80 * quarter + 20 * (line >> 3) + (line & 3)).astype(F32)
    pupil_row = jnp.concatenate([base + 4.0 * rr for rr in range(5)], axis=0)
    spot = iota((1, 256), 1)
    screen_row = (ring * 32 + 8 * ((spot >> 2) & 3) + 4 * (spot >> 7) + (spot & 3)).astype(F32)
    tops = [jnp.where(star == 0, row_ref[frame, 0:1, :], row_ref[frame, 1:2, :]) for frame in range(2)]
    parts = [top >> 4 for top in tops] + [top & 15 for top in tops] + [bin_ref[...].reshape(1, 16)]
    line16 = iota((8, 16), 0)
    packed = jnp.zeros((8, 16), F32)
    for n, part in enumerate(parts):
        packed = jnp.where(line16 == n, part.astype(F32), packed)
    packed = packed.astype(BF16)
    sums = [None, None]
    for layer in range(2):
        pick = (iota((16, 256), 0) == 2 * ((iota((16, 256), 1) >> 4) & 7) + layer).astype(F32).astype(BF16)
        lanes = jnp.dot(packed, pick, preferred_element_type=F32)
        scaled = pupil_row * (1.0 - lanes[4:5] * 0.03125)
        for frame in range(2):
            offset = screen_row - (16.0 * lanes[frame : frame + 1] + lanes[2 + frame : 3 + frame])
            weights = tent(offset - scaled)
            term = jnp.dot(weights, rights[layer], preferred_element_type=F32)
            sums[frame] = term if layer == 0 else sums[frame] + term
    sums = [total[:, :128] + total[:, 128:] for total in sums]
    merged = jnp.where(iota((160, 128), 1) < 56, sums[0], sums[1])
    lane = iota((8, 128), 1)
    cell = jnp.where(lane < 56, lane, lane - 56)
    kind = jnp.where(cell < 32, cell >> 3, block >> 1)
    for t in range(4):
        pieces = [merged[rr * 32 + t * 8 : rr * 32 + t * 8 + 8] for rr in range(5)]
        for zl in range(4):
            here, after = pieces[zl], pieces[zl + 1]
            first = jnp.where(kind < zl, after, here)
            second = jnp.where(cell < 48, pltpu.roll(after, 40 - 8 * zl, axis=1), pltpu.roll(after, 16, axis=1))
            value = jnp.where(cell < 40, first, second)
            last = pltpu.roll(jnp.broadcast_to(value[7:8], (8, 128)), 16, axis=1, stride=16, stride_axis=0)
            value = jnp.where(lane < 112, value, last)
            for n in range(7):
                out_ref[t * 4 + zl, n] = value[n : n + 1]
    scratch[...] = jnp.ones((16, 128), F32)
    scratch[:, 0:25] = light_ref[...]
    wide = scratch[...]
    inside = iota((16, 128), 1)
    scratch[...] = jnp.where((inside >= 64) & (inside < 89), pltpu.roll(wide, 64, axis=1), wide)
    for q in range(4):
        top = (q % 2) * 4
        light_out[q // 2, top : top + 4, :] = scratch[pl.ds(q, 4, stride=4), :]


def spread_kernel(got_ref, out_ref, scratch):
    total = jnp.sum(got_ref[...], axis=0)
    scratch[...] = jnp.zeros((16, 128), F32)
    for n in range(7):
        scratch[n : n + 1] = total[n]
        scratch[14 - n : 15 - n] = total[n]
    total = scratch[0:8]
    row = iota((8, 128), 0)
    lane = iota((8, 128), 1)
    ends = pltpu.roll(scratch[8:16], 16, axis=1, stride=16, stride_axis=0)
    last = jnp.sum(jnp.where((lane >> 4) == row, ends, 0.0), axis=0, keepdims=True)
    total = jnp.where(row == 7, last, total)
    total = jnp.where(lane < 64, total, pltpu.roll(total, 8, axis=1))
    for to in range(8):
        top = (to // 4) * 4
        out_ref[to] = total[top : top + 4]


def slopes_kernel(got_ref, light_ref, recon_ref, slopes_ref, out_ref, scratch):
    zl = lax.axis_index("zl")
    row = iota((8, 128), 0)
    lane = iota((8, 128), 1)
    for source in range(8):
        block = got_ref[source]
        for q in range(4):
            scratch[source, 4 * q : 4 * q + 4] = block if q == 0 else pltpu.roll(block, 128 - q, axis=1)
    cell16 = iota((16, 128), 1) & 63
    phase = jnp.zeros((16, 128), F32)
    flat_start = 100 * zl + 25 * ylc_index()
    for five in range(5):
        flat = flat_start + 5 * five
        lens_row = (flat * 205) >> 14
        lens_col = flat - 80 * lens_row
        kind = (lens_col * 205) >> 12
        start = lens_col - 20 * kind
        first = lens_row == zl + (kind < zl).astype(I32)
        regular_place = jnp.where(first, 8 * kind, 40)
        more_place = jnp.where(first, 32, 48)
        inner = start < 15
        for j in range(5):
            n = 5 * five + j
            index = start + j
            source = index >> 1
            place = regular_place + 4 * (index & 1)
            if j > 0:
                source = jnp.where(inner, source, 2 * kind + (j - 1) // 2)
                place = jnp.where(inner, place, more_place + 4 * ((j - 1) % 2))
            phase = jnp.where(cell16 == n, pltpu.roll(scratch[source], (n + 128 - place) & 127, axis=1), phase)
    phases = [phase[0:8], phase[8:16]]
    re, im = [], []
    for h in range(2):
        light = light_ref[h]
        re.append(light * jnp.cos(phases[h]))
        im.append(light * jnp.sin(phases[h]))
    power = re[0] * re[0] + im[0] * im[0] + re[1] * re[1] + im[1] * im[1]
    flux = jnp.sum(power, axis=0, keepdims=True)
    along_p = -4.0 * power
    pixel = row & 3
    for h in range(2):
        for d in range(1, 4):
            back_re = pltpu.roll(re[h], d, axis=0)
            back_im = pltpu.roll(im[h], d, axis=0)
            same = re[h] * back_re + im[h] * back_im
            cross = im[h] * back_re - re[h] * back_im
            sign = -8.0 if d % 2 == 0 else 8.0
            term = sign * same + (4.0 * LAG[d - 1]) * cross
            along_p = along_p + jnp.where(pixel >= d, term, 0.0)
    swap_re = [pltpu.roll(x, 4, axis=0) for x in re]
    swap_im = [pltpu.roll(x, 4, axis=0) for x in im]

    def term_of(to_re, to_im, from_re, from_im, d):
        same = to_re * from_re + to_im * from_im
        cross = to_im * from_re - to_re * from_im
        sign = -8.0 if d % 2 == 0 else 8.0
        return sign * same + (4.0 * LAG[d - 1]) * cross

    along_q = -4.0 * power
    upper = row >= 4
    for h in range(2):
        along_q = along_q + jnp.where(upper, term_of(re[h], im[h], swap_re[h], swap_im[h], 1), 0.0)
    along_q = along_q + term_of(re[1], im[1], re[0], im[0], 2)
    near = term_of(re[1], im[1], swap_re[0], swap_im[0], 1)
    far = term_of(re[1], im[1], swap_re[0], swap_im[0], 3)
    along_q = along_q + jnp.where(upper, far, near)
    scale = 0.125 / flux
    slope_p = jnp.sum(along_p, axis=0, keepdims=True) * scale
    slope_q = jnp.sum(along_q, axis=0, keepdims=True) * scale
    pair = jnp.where(row == 0, slope_p, slope_q)
    compact = [pair, pltpu.roll(pair, 64, axis=1)]
    for frame in range(2):
        slopes_ref[frame] = compact[frame]
    total = jnp.zeros((8, ACTUATORS), F32)
    for axis in range(2):
        left = jnp.where(row == 0, compact[0][axis : axis + 1], compact[1][axis : axis + 1])
        left = left[:, 0:25].astype(BF16)
        total = total + jnp.dot(left, recon_ref[axis], preferred_element_type=F32)
    for j in range(32):
        start = 384 * (j % 16)
        width = min(384, ACTUATORS - start)
        if width < 384:
            out_ref[j] = jnp.zeros((1, 384), F32)
        out_ref[j, :, 0:width] = total[j // 16 : j // 16 + 1, start : start + width]


def sum_kernel(got_ref, out_ref):
    total = jnp.sum(got_ref[...], axis=0)
    for i in range(out_ref.shape[0]):
        out_ref[i] = total


def clip_kernel(got_ref, code_ref, slopes_ref, slopes_out, out_ref):
    slopes_out[...] = slopes_ref[:, 0:2, 0:25]
    for j in range(16):
        start = 384 * j
        width = min(384, ACTUATORS - start)
        limit = code_ref[start : start + width].reshape(1, width).astype(F32) * 0.125
        first = jnp.clip(0.5 * got_ref[j][:, 0:width], -limit, limit)
        second = jnp.clip(first + 0.5 * got_ref[16 + j][:, 0:width], -limit, limit)
        out_ref[0:1, start : start + width] = first
        out_ref[1:2, start : start + width] = second


def call(body, outs, specs, *args, scratch=(), name=None):
    return pl.pallas_call(
        body,
        out_shape=outs,
        in_specs=specs,
        out_specs=jax.tree.map(lambda _: VMEM, outs),
        scratch_shapes=list(scratch),
        compiler_params=pltpu.CompilerParams(vmem_limit_bytes=16 * 1024 * 1024),
        name=name,
    )(*args)


def exchange(value, axes):
    return lax.all_to_all(value, axes, 0, 0, tiled=True)


def shards(screens, row_offset, col_offset, layer_bin, illumination, reconstructor, sat_code):
    shape = jax.ShapeDtypeStruct
    row_offset = jnp.transpose(row_offset, (0, 2, 1))
    cols = call(columns_kernel, shape((32, 3, 4, 128), F32), [VMEM, VMEM, VMEM], col_offset, layer_bin, screens, name="columns")
    cols = exchange(cols, PLANE)
    pupil, light = call(
        rows_kernel,
        (shape((16, 7, 1, 128), F32), shape((2, 8, 128), F32)),
        [VMEM, VMEM, VMEM, VMEM],
        row_offset,
        layer_bin,
        illumination,
        cols,
        scratch=[pltpu.VMEM((16, 128), F32)],
        name="rows",
    )
    pupil = exchange(pupil, RING)
    owned = call(spread_kernel, shape((8, 4, 128), F32), [VMEM], pupil, scratch=[pltpu.VMEM((16, 128), F32)], name="spread")
    owned = exchange(owned, EIGHT)
    owned, reconstructor = lax.optimization_barrier((owned, reconstructor))
    slopes, updates = call(
        slopes_kernel,
        (shape((2, 8, 128), F32), shape((32, 1, 384), F32)),
        [VMEM, VMEM, VMEM],
        owned,
        light,
        reconstructor,
        scratch=[pltpu.VMEM((8, 16, 128), F32)],
        name="slopes",
    )
    updates = exchange(updates, PLANE)
    updates = call(sum_kernel, shape((16, 1, 384), F32), [VMEM], updates, name="sum_plane")
    updates = exchange(updates, RING)
    updates = call(sum_kernel, shape((32, 1, 384), F32), [VMEM], updates, name="sum_ring")
    updates = exchange(updates, PLANE)
    return call(
        clip_kernel,
        (shape((2, 2, 25), F32), shape((2, ACTUATORS), F32)),
        [VMEM, VMEM, VMEM],
        updates,
        sat_code,
        slopes,
        name="clip",
    )


def solution(mesh):
    fine = Mesh(mesh.devices.reshape(SIZES), NAMES)
    placed = (
        P(ALT, STRIP, None),
        P(),
        P(),
        P(),
        P(None, ALT + STRIP),
        P(None, ALT + STRIP, None),
        P(),
    )
    return jax.shard_map(
        shards,
        mesh=fine,
        in_specs=placed,
        out_specs=(P(None, None, ALT + STRIP), P()),
        check_vma=False,
    )
```

```python
import jax
import jax.numpy as jnp
from jax import lax
from jax.experimental import pallas as pl
from jax.experimental.pallas import tpu as pltpu
from jax.sharding import Mesh, PartitionSpec as P

ACTUATORS = 6000
F32 = jnp.float32
BF16 = jnp.bfloat16
I32 = jnp.int32

NAMES = ("xh", "xl", "yh", "zh", "zl", "yl", "co")
SIZES = (2, 2, 2, 4, 4, 2, 2)
ALT = ("xh", "xl", "yh")
STRIP = ("zh", "zl", "yl", "co")
PLANE = ("xh", "xl", "yh", "yl", "co")
EIGHT = ("xl", "yl", "co")
RING = ("zh", "zl")

ROOT = 2.0**0.5
LAG = (2.0 + 2.0 * ROOT, -2.0, 2.0 * ROOT - 2.0)

VMEM = pl.BlockSpec(memory_space=pltpu.VMEM)


def iota(shape, dim):
    return lax.broadcasted_iota(I32, shape, dim)


def tent(offset):
    return jnp.maximum(BF16(0.0), BF16(1.0) - jnp.abs(offset.astype(BF16)))


def alt_index():
    return lax.axis_index("xh") * 4 + lax.axis_index("xl") * 2 + lax.axis_index("yh")


def ylc_index():
    return lax.axis_index("yl") * 2 + lax.axis_index("co")


def block_index():
    return lax.axis_index("xl") * 4 + ylc_index()


def columns_kernel(col_ref, bin_ref, screen_ref, out_ref):
    alt = alt_index()
    lane = iota((1, 512), 1)
    block = lane >> 6
    part = (lane & 63) >> 2
    more = 20 * (block >> 1) + 16 + 2 * (block & 1)
    lenslet = jnp.where(part < 8, 20 * (part >> 1) + 2 * block, more) + (part & 1)
    column = (4 * lenslet + (lane & 3)).astype(F32)
    position = iota((320, 512), 0).astype(F32)
    results = []
    bins = bin_ref[...].reshape(1, 16)
    lefts = [col_ref[frame, pl.ds(2 * alt, 2), :] for frame in range(2)]
    for layer in range(2):
        chosen = jnp.where(iota((1, 16), 1) == 2 * alt + layer, bins, 0).astype(F32)
        shrink = 1.0 - jnp.sum(chosen, axis=1, keepdims=True) * 0.03125
        weights = tent(position - column * shrink)
        rows = screen_ref[layer].astype(F32)
        parts = []
        for frame in range(2):
            for star in range(2):
                turned = pltpu.roll(rows, (512 - lefts[frame][layer, star]) & 511, axis=1)
                parts.append(turned[:, :320])
        stacked = jnp.concatenate(parts, axis=0).astype(BF16)
        results.append(jnp.dot(stacked, weights, preferred_element_type=F32))
    lane = iota((8, 128), 1)
    for star in range(2):
        for block in range(8):
            start = (block // 2) * 128
            back = (block % 2) * 64

            def piece(layer, frame, to):
                top = frame * 16 + star * 8
                value = results[layer][top : top + 8, start : start + 128]
                shift = (to - back) % 128
                return value if shift == 0 else pltpu.roll(value, shift, axis=1)

            main = jnp.where(lane < 40, piece(0, 0, 0), jnp.where(lane < 80, piece(0, 1, 40), piece(1, 0, 80)))
            rest = jnp.where(lane[0:4] < 64, piece(1, 1, 0)[0:4], piece(1, 1, 64)[4:8])
            for yh in range(2):
                to = star * 16 + (block // 4) * 8 + yh * 4 + block % 4
                out_ref[to, 0] = main[0:4]
                out_ref[to, 1] = main[4:8]
                out_ref[to, 2] = rest


def rows_kernel(row_ref, bin_ref, light_ref, got_ref, out_ref, light_out, scratch):
    star = lax.axis_index("xh")
    block = block_index()
    ring = lax.axis_index("zh") * 4 + lax.axis_index("zl")
    main = jnp.concatenate([got_ref[:, half].reshape(128, 128) for half in range(2)], axis=0)
    rest = got_ref[:, 2].reshape(128, 128)
    rest = jnp.concatenate([pltpu.roll(rest, 56, axis=1), pltpu.roll(rest, 120, axis=1)], axis=0)
    left_half = iota((256, 128), 1) < 56
    rights = []
    for value in (
        jnp.where(left_half, main, pltpu.roll(main, 16, axis=1)),
        jnp.where(left_half, pltpu.roll(main, 48, axis=1), rest),
    ):
        high = value.astype(BF16)
        rights.append(jnp.concatenate([high, (value - high.astype(F32)).astype(BF16)], axis=1))
    line = iota((32, 1), 0)
    quarter = 2 * ((line >> 2) & 1) + lax.axis_index("yh")
    base = (80 * quarter + 20 * (line >> 3) + (line & 3)).astype(F32)
    pupil_row = jnp.concatenate([base + 4.0 * rr for rr in range(5)], axis=0)
    spot = iota((1, 256), 1)
    screen_row = (ring * 32 + 8 * ((spot >> 2) & 3) + 4 * (spot >> 7) + (spot & 3)).astype(F32)
    tops = [jnp.where(star == 0, row_ref[frame, 0:1, :], row_ref[frame, 1:2, :]) for frame in range(2)]
    parts = [top >> 4 for top in tops] + [top & 15 for top in tops] + [bin_ref[...].reshape(1, 16)]
    line16 = iota((8, 16), 0)
    packed = jnp.zeros((8, 16), F32)
    for n, part in enumerate(parts):
        packed = jnp.where(line16 == n, part.astype(F32), packed)
    packed = packed.astype(BF16)
    sums = [None, None]
    for layer in range(2):
        pick = (iota((16, 256), 0) == 2 * ((iota((16, 256), 1) >> 4) & 7) + layer).astype(F32).astype(BF16)
        lanes = jnp.dot(packed, pick, preferred_element_type=F32)
        scaled = pupil_row * (1.0 - lanes[4:5] * 0.03125)
        for frame in range(2):
            offset = screen_row - (16.0 * lanes[frame : frame + 1] + lanes[2 + frame : 3 + frame])
            weights = tent(offset - scaled)
            term = jnp.dot(weights, rights[layer], preferred_element_type=F32)
            sums[frame] = term if layer == 0 else sums[frame] + term
    sums = [total[:, :128] + total[:, 128:] for total in sums]
    merged = jnp.where(iota((160, 128), 1) < 56, sums[0], sums[1])
    lane = iota((8, 128), 1)
    cell = jnp.where(lane < 56, lane, lane - 56)
    kind = jnp.where(cell < 32, cell >> 3, block >> 1)
    for t in range(4):
        pieces = [merged[rr * 32 + t * 8 : rr * 32 + t * 8 + 8] for rr in range(5)]
        for zl in range(4):
            here, after = pieces[zl], pieces[zl + 1]
            first = jnp.where(kind < zl, after, here)
            second = jnp.where(cell < 48, pltpu.roll(after, 40 - 8 * zl, axis=1), pltpu.roll(after, 16, axis=1))
            value = jnp.where(cell < 40, first, second)
            last = pltpu.roll(jnp.broadcast_to(value[7:8], (8, 128)), 16, axis=1, stride=16, stride_axis=0)
            value = jnp.where(lane < 112, value, last)
            for n in range(7):
                out_ref[t * 4 + zl, n] = value[n : n + 1]
    scratch[...] = jnp.ones((16, 128), F32)
    scratch[:, 0:25] = light_ref[...]
    wide = scratch[...]
    inside = iota((16, 128), 1)
    scratch[...] = jnp.where((inside >= 64) & (inside < 89), pltpu.roll(wide, 64, axis=1), wide)
    for q in range(4):
        top = (q % 2) * 4
        light_out[q // 2, top : top + 4, :] = scratch[pl.ds(q, 4, stride=4), :]


def spread_kernel(got_ref, out_ref, scratch):
    total = jnp.sum(got_ref[...], axis=0)
    scratch[...] = jnp.zeros((16, 128), F32)
    for n in range(7):
        scratch[n : n + 1] = total[n]
        scratch[14 - n : 15 - n] = total[n]
    total = scratch[0:8]
    row = iota((8, 128), 0)
    lane = iota((8, 128), 1)
    ends = pltpu.roll(scratch[8:16], 16, axis=1, stride=16, stride_axis=0)
    last = jnp.sum(jnp.where((lane >> 4) == row, ends, 0.0), axis=0, keepdims=True)
    total = jnp.where(row == 7, last, total)
    total = jnp.where(lane < 64, total, pltpu.roll(total, 8, axis=1))
    for to in range(8):
        top = (to // 4) * 4
        out_ref[to] = total[top : top + 4]


def slopes_kernel(got_ref, light_ref, recon_ref, slopes_ref, out_ref, scratch):
    zl = lax.axis_index("zl")
    row = iota((8, 128), 0)
    lane = iota((8, 128), 1)
    for source in range(8):
        block = got_ref[source]
        for q in range(4):
            scratch[source, 4 * q : 4 * q + 4] = block if q == 0 else pltpu.roll(block, 128 - q, axis=1)
    cell16 = iota((16, 128), 1) & 63
    phase = jnp.zeros((16, 128), F32)
    flat_start = 100 * zl + 25 * ylc_index()
    for five in range(5):
        flat = flat_start + 5 * five
        lens_row = (flat * 205) >> 14
        lens_col = flat - 80 * lens_row
        kind = (lens_col * 205) >> 12
        start = lens_col - 20 * kind
        first = lens_row == zl + (kind < zl).astype(I32)
        regular_place = jnp.where(first, 8 * kind, 40)
        more_place = jnp.where(first, 32, 48)
        inner = start < 15
        for j in range(5):
            n = 5 * five + j
            index = start + j
            source = index >> 1
            place = regular_place + 4 * (index & 1)
            if j > 0:
                source = jnp.where(inner, source, 2 * kind + (j - 1) // 2)
                place = jnp.where(inner, place, more_place + 4 * ((j - 1) % 2))
            phase = jnp.where(cell16 == n, pltpu.roll(scratch[source], (n + 128 - place) & 127, axis=1), phase)
    phases = [phase[0:8], phase[8:16]]
    re, im = [], []
    for h in range(2):
        light = light_ref[h]
        re.append(light * jnp.cos(phases[h]))
        im.append(light * jnp.sin(phases[h]))
    power = re[0] * re[0] + im[0] * im[0] + re[1] * re[1] + im[1] * im[1]
    flux = jnp.sum(power, axis=0, keepdims=True)
    along_p = -4.0 * power
    pixel = row & 3
    for h in range(2):
        for d in range(1, 4):
            back_re = pltpu.roll(re[h], d, axis=0)
            back_im = pltpu.roll(im[h], d, axis=0)
            same = re[h] * back_re + im[h] * back_im
            cross = im[h] * back_re - re[h] * back_im
            sign = -8.0 if d % 2 == 0 else 8.0
            term = sign * same + (4.0 * LAG[d - 1]) * cross
            along_p = along_p + jnp.where(pixel >= d, term, 0.0)
    swap_re = [pltpu.roll(x, 4, axis=0) for x in re]
    swap_im = [pltpu.roll(x, 4, axis=0) for x in im]

    def term_of(to_re, to_im, from_re, from_im, d):
        same = to_re * from_re + to_im * from_im
        cross = to_im * from_re - to_re * from_im
        sign = -8.0 if d % 2 == 0 else 8.0
        return sign * same + (4.0 * LAG[d - 1]) * cross

    along_q = -4.0 * power
    upper = row >= 4
    for h in range(2):
        along_q = along_q + jnp.where(upper, term_of(re[h], im[h], swap_re[h], swap_im[h], 1), 0.0)
    along_q = along_q + term_of(re[1], im[1], re[0], im[0], 2)
    near = term_of(re[1], im[1], swap_re[0], swap_im[0], 1)
    far = term_of(re[1], im[1], swap_re[0], swap_im[0], 3)
    along_q = along_q + jnp.where(upper, far, near)
    scale = 0.125 / flux
    slope_p = jnp.sum(along_p, axis=0, keepdims=True) * scale
    slope_q = jnp.sum(along_q, axis=0, keepdims=True) * scale
    pair = jnp.where(row == 0, slope_p, slope_q)
    compact = [pair, pltpu.roll(pair, 64, axis=1)]
    for frame in range(2):
        slopes_ref[frame] = compact[frame]
    total = jnp.zeros((8, ACTUATORS), F32)
    for axis in range(2):
        left = jnp.where(row == 0, compact[0][axis : axis + 1], compact[1][axis : axis + 1])
        left = left[:, 0:25].astype(BF16)
        total = total + jnp.dot(left, recon_ref[axis], preferred_element_type=F32)
    for j in range(32):
        start = 384 * (j % 16)
        width = min(384, ACTUATORS - start)
        if width < 384:
            out_ref[j] = jnp.zeros((1, 384), F32)
        out_ref[j, :, 0:width] = total[j // 16 : j // 16 + 1, start : start + width]


def sum_kernel(got_ref, out_ref):
    total = jnp.sum(got_ref[...], axis=0)
    for i in range(out_ref.shape[0]):
        out_ref[i] = total


def clip_kernel(got_ref, code_ref, slopes_ref, slopes_out, out_ref):
    slopes_out[...] = slopes_ref[:, 0:2, 0:25]
    for j in range(16):
        start = 384 * j
        width = min(384, ACTUATORS - start)
        limit = code_ref[start : start + width].reshape(1, width).astype(F32) * 0.125
        first = jnp.clip(0.5 * got_ref[j][:, 0:width], -limit, limit)
        second = jnp.clip(first + 0.5 * got_ref[16 + j][:, 0:width], -limit, limit)
        out_ref[0:1, start : start + width] = first
        out_ref[1:2, start : start + width] = second


def call(body, outs, specs, *args, scratch=(), name=None):
    return pl.pallas_call(
        body,
        out_shape=outs,
        in_specs=specs,
        out_specs=jax.tree.map(lambda _: VMEM, outs),
        scratch_shapes=list(scratch),
        compiler_params=pltpu.CompilerParams(vmem_limit_bytes=16 * 1024 * 1024),
        name=name,
    )(*args)


def exchange(value, axes):
    return lax.all_to_all(value, axes, 0, 0, tiled=True)


def shards(screens, row_offset, col_offset, layer_bin, illumination, reconstructor, sat_code):
    shape = jax.ShapeDtypeStruct
    row_offset = jnp.transpose(row_offset, (0, 2, 1))
    cols = call(columns_kernel, shape((32, 3, 4, 128), F32), [VMEM, VMEM, VMEM], col_offset, layer_bin, screens, name="columns")
    cols = exchange(cols, PLANE)
    pupil, light = call(
        rows_kernel,
        (shape((16, 7, 1, 128), F32), shape((2, 8, 128), F32)),
        [VMEM, VMEM, VMEM, VMEM],
        row_offset,
        layer_bin,
        illumination,
        cols,
        scratch=[pltpu.VMEM((16, 128), F32)],
        name="rows",
    )
    pupil = exchange(pupil, RING)
    owned = call(spread_kernel, shape((8, 4, 128), F32), [VMEM], pupil, scratch=[pltpu.VMEM((16, 128), F32)], name="spread")
    owned = exchange(owned, EIGHT)
    owned, reconstructor = lax.optimization_barrier((owned, reconstructor))
    slopes, updates = call(
        slopes_kernel,
        (shape((2, 8, 128), F32), shape((32, 1, 384), F32)),
        [VMEM, VMEM, VMEM],
        owned,
        light,
        reconstructor,
        scratch=[pltpu.VMEM((8, 16, 128), F32)],
        name="slopes",
    )
    updates = exchange(updates, PLANE)
    updates = call(sum_kernel, shape((16, 1, 384), F32), [VMEM], updates, name="sum_plane")
    updates = exchange(updates, RING)
    updates = call(sum_kernel, shape((32, 1, 384), F32), [VMEM], updates, name="sum_ring")
    updates = exchange(updates, PLANE)
    return call(
        clip_kernel,
        (shape((2, 2, 25), F32), shape((2, ACTUATORS), F32)),
        [VMEM, VMEM, VMEM],
        updates,
        sat_code,
        slopes,
        name="clip",
    )


def solution(mesh):
    fine = Mesh(mesh.devices.reshape(SIZES), NAMES)
    placed = (
        P(ALT, STRIP, None),
        P(),
        P(),
        P(),
        P(None, ALT + STRIP),
        P(None, ALT + STRIP, None),
        P(),
    )
    return jax.shard_map(
        shards,
        mesh=fine,
        in_specs=placed,
        out_specs=(P(None, None, ALT + STRIP), P()),
        check_vma=False,
    )
```
